512 devices in a mesh: ctx: 128 (over z, y, x_hi), tp: 4 (over x_lo, core).
Axes of the slice: x: 4 (x_hi: 2, x_lo: 2; x = x_hi * 2 + x_lo), y: 4, z: 16, core: 2. Of those that a mesh axis runs over, the one named last changes fastest.
Arguments:
- query_heads: bfloat16 [16384, 4096], P('ctx', 'tp'), may hold values from -16 to 16
- key_heads_wide: bfloat16 [16384, 512], P(('ctx', 'tp')), may hold values from -16 to 16
- value_heads_wide: bfloat16 [16384, 512], P(('ctx', 'tp')), may hold values from -6 to 6
- grad_output: bfloat16 [16384, 4096], P('ctx', 'tp'), may hold values from -48 to 48
Outputs:
- grad_query: float32 [16384, 4096], P('ctx', 'tp')
- key_gradient: float32 [16384, 512], P(('ctx', 'tp'))
- value_gradient: float32 [16384, 512], P(('ctx', 'tp'))
The draws below stay inside these ranges and needn't reach their ends.
All inputs are finite; a program needn't handle non-finite values.
Results may differ from the reference program's by a relative error of at most 0.007.
Values may be sent and summed in bfloat16 or wider, within the bound.
No kernel may reach another device: no remote copies, remote signals or barrier semaphores. Data moves between devices by JAX's collectives and lax.ppermute only.
A program may use at most 64 MiB of HBM per device.

```python
import math
import jax
import jax.numpy as jnp
from jax import lax

HEAD_SIZE = 128
QUERY_HEADS = 32
KEY_VALUE_HEADS = 4
SEQUENCE_TOKENS = 16384
GROUP = 4096
HALF_ROLL_SIZE = 2048


def draw_key_heads_wide(key, part):
    key = jax.random.fold_in(key, 1)
    unshifted_heads = jnp.clip(jax.random.normal(key, (SEQUENCE_TOKENS, KEY_VALUE_HEADS * HEAD_SIZE), jnp.float32), -6.0, 6.0)
    return unshifted_heads.astype(jnp.bfloat16)


def draw_query_heads(key, part):
    key = jax.random.fold_in(key, 2)
    unshifted_heads = jnp.clip(jax.random.normal(key, (SEQUENCE_TOKENS, QUERY_HEADS * HEAD_SIZE), jnp.float32), -6.0, 6.0)
    return unshifted_heads.astype(jnp.bfloat16)


def block_scale(rng, extent, pieces, low, high):
    gain = 1.0
    for dim, shards_of in pieces:
        draws = jax.random.uniform(jax.random.fold_in(jax.random.fold_in(rng, 6), dim), (shards_of,), jnp.float32, low / len(pieces), high / len(pieces))
        gain = gain * jnp.repeat(jnp.exp(draws), extent[dim] // shards_of).reshape((-1,) + (1,) * (len(extent) - 1 - dim))
    return gain


def bell_draw(own_key, shape, spread, most, shards=(), kind=jnp.bfloat16):
    entries = jax.random.normal(own_key, shape, jnp.float32) * spread
    if len(shards) > 0:
        entries = block_scale(own_key, shape, shards, -0.22, 0.18) * entries
    return jnp.clip(entries, min=-most, max=most).astype(kind)


def setup_inputs(seed: int = 0) -> dict:
    streams_of = jax.random.split(jax.random.key(seed), 5)
    return {
        "query_heads": draw_query_heads(jax.random.fold_in(streams_of[4], 71), 0),
        "key_heads_wide": draw_key_heads_wide(jax.random.fold_in(streams_of[4], 71), 0),
        "value_heads_wide": bell_draw(streams_of[2], (SEQUENCE_TOKENS, KEY_VALUE_HEADS * HEAD_SIZE), 1.0, 6.0, ((0, 512),)),
        "grad_output": bell_draw(streams_of[3], (SEQUENCE_TOKENS, QUERY_HEADS * HEAD_SIZE), 8.0, 48.0, ((0, 128), (1, 4))),
    }


def group_grads(query_part, key_part, value_part, grad_part):
    length = query_part.shape[0]
    score_scale = 1.0 / math.sqrt(query_part.shape[1])
    scores = jnp.dot(query_part, key_part.T, preferred_element_type=jnp.float32) * score_scale
    row_index = lax.broadcasted_iota(jnp.int32, (length, length), 0)
    col_index = lax.broadcasted_iota(jnp.int32, (length, length), 1)
    visible = col_index <= row_index
    scores = jnp.where(visible, scores, -jnp.inf)
    highest = lax.optimization_barrier(jnp.max(scores, axis=1, keepdims=True))
    totals = lax.optimization_barrier(jnp.sum(jnp.exp(scores - highest), axis=1, keepdims=True))
    log_norm = highest + jnp.log(totals)
    slopes = jnp.dot(grad_part, value_part.T, preferred_element_type=jnp.float32)
    soft_weights = jnp.exp(scores - log_norm)
    centre = lax.optimization_barrier(jnp.sum(soft_weights * slopes, axis=1, keepdims=True))
    soft_low = soft_weights.astype(jnp.bfloat16)
    score_grad = (soft_weights * (slopes - centre)).astype(jnp.bfloat16)
    query_grad = jnp.dot(score_grad, key_part, preferred_element_type=jnp.float32) * score_scale
    key_grad = jnp.dot(score_grad.T, query_part, preferred_element_type=jnp.float32) * score_scale
    value_grad = jnp.dot(soft_low.T, grad_part, preferred_element_type=jnp.float32)
    return (query_grad, key_grad, value_grad)

def head_grads(query_one, key_one, value_one, grad_one, roll_amount):
    parts = tuple((jnp.roll(array, -roll_amount, axis=0).reshape(SEQUENCE_TOKENS // GROUP, GROUP, HEAD_SIZE) for array in (query_one, key_one, value_one, grad_one)))
    results = lax.map(lambda items: group_grads(*items), parts)
    return tuple((jnp.roll(result.reshape(SEQUENCE_TOKENS, HEAD_SIZE), roll_amount, axis=0) for result in results))

def reference(query_heads, key_heads_wide, value_heads_wide, grad_output):
    query_heads_per_group = QUERY_HEADS // KEY_VALUE_HEADS
    query_split = query_heads.reshape(SEQUENCE_TOKENS, QUERY_HEADS, HEAD_SIZE)
    grad_split = grad_output.reshape(SEQUENCE_TOKENS, QUERY_HEADS, HEAD_SIZE)
    key_separated = key_heads_wide.reshape(SEQUENCE_TOKENS, KEY_VALUE_HEADS, HEAD_SIZE)
    value_separated = value_heads_wide.reshape(SEQUENCE_TOKENS, KEY_VALUE_HEADS, HEAD_SIZE)
    query_list, key_pieces, value_pieces = ([], [], [])
    for shared_head in range(KEY_VALUE_HEADS):
        roll_amount = HALF_ROLL_SIZE if shared_head >= KEY_VALUE_HEADS // 2 else 0
        key_one = key_separated[:, shared_head]
        value_one = value_separated[:, shared_head]

        def visit(loop_state, offset, shared_head=shared_head, roll_amount=roll_amount, key_one=key_one, value_one=value_one):
            index = shared_head * query_heads_per_group + offset
            query_one = lax.dynamic_index_in_dim(query_split, index, 1, keepdims=False)
            grad_one = lax.dynamic_index_in_dim(grad_split, index, 1, keepdims=False)
            query_grad, key_grad, value_grad = head_grads(query_one, key_one, value_one, grad_one, roll_amount)
            return ((loop_state[0] + key_grad, loop_state[1] + value_grad), query_grad)
        zeros = jnp.zeros((SEQUENCE_TOKENS, HEAD_SIZE), jnp.float32)
        (key_total, value_total), query_grads = lax.scan(visit, (zeros, zeros), jnp.arange(query_heads_per_group, dtype=jnp.int32))
        query_list.append(query_grads)
        key_pieces.append(key_total)
        value_pieces.append(value_total)
    grad_query = jnp.stack(query_list).transpose(2, 0, 1, 3).reshape(SEQUENCE_TOKENS, QUERY_HEADS * HEAD_SIZE)
    key_gradient = jnp.stack(key_pieces).transpose(1, 0, 2).reshape(SEQUENCE_TOKENS, KEY_VALUE_HEADS * HEAD_SIZE)
    value_gradient = jnp.stack(value_pieces).transpose(1, 0, 2).reshape(SEQUENCE_TOKENS, KEY_VALUE_HEADS * HEAD_SIZE)
    return (grad_query, key_gradient, value_gradient)
```

```python
import functools
import math

import jax
import jax.numpy as jnp
from jax import lax
from jax.experimental import pallas as pl
from jax.experimental.pallas import tpu as pltpu
from jax.sharding import PartitionSpec as P

HEAD_SIZE = 128
GROUPS = 4
SLABS = 4
KEYS = 512
ROWS = 512
AXES = ("ctx", "tp")
BF16, F32 = jnp.bfloat16, jnp.float32


def product(a, b):
    return jnp.dot(a, b, preferred_element_type=F32)


def attention_kernel(
    rank_ref, q_ref, do_ref, kv_ref, dq_ref, dkv_ref,
    q_rows, do_rows, q_cols, do_cols, k_cols, weights, slopes, maxima, total,
):
    tokens = q_ref.shape[0]
    heads = q_ref.shape[1] // HEAD_SIZE
    blocks, slabs = kv_ref.shape[0], kv_ref.shape[1]
    per_step = KEYS // tokens
    steps_per_slab = blocks // per_step
    rank = rank_ref[0]
    steps = lax.div(rank, jnp.int32(per_step)) + 1
    scale = 1.0 / math.sqrt(HEAD_SIZE)

    for h in range(heads):
        across = slice(h * HEAD_SIZE, (h + 1) * HEAD_SIZE)
        down = slice(h * tokens, (h + 1) * tokens)
        q_rows[down, :] = q_ref[:, across]
        do_rows[down, :] = do_ref[:, across]
        q_cols[:, down] = q_ref[:, across].T
        do_cols[:, down] = do_ref[:, across].T

    def block(step, column):
        slab = lax.div(step, jnp.int32(steps_per_slab))
        first = lax.rem(step, jnp.int32(steps_per_slab)) * per_step
        part = kv_ref[pl.ds(first, per_step), slab, :, column * HEAD_SIZE : (column + 1) * HEAD_SIZE]
        return part.reshape(KEYS, HEAD_SIZE)

    @pl.loop(0, steps)
    def _(step):
        k_cols[:, pl.ds(pl.multiple_of(step * KEYS, KEYS), KEYS)] = block(step, 0).T

    for tile in range(heads * tokens // ROWS):
        rows = slice(tile * ROWS, (tile + 1) * ROWS)

        def statistics(step, carry, masked):
            highest, norm, weighted = carry
            first = pl.multiple_of(step * KEYS, KEYS)
            scores = product(block(step, 0), q_cols[:, rows]) * (scale * math.log2(math.e))
            if masked:
                key = lax.broadcasted_iota(jnp.int32, (KEYS, ROWS), 0) + (first - rank * tokens)
                query = lax.rem(lax.broadcasted_iota(jnp.int32, (KEYS, ROWS), 1), tokens)
                scores = jnp.where(key <= query, scores, -jnp.inf)
            higher = jnp.maximum(highest, jnp.max(scores, axis=0, keepdims=True))
            weight = jnp.exp2(scores - higher)
            factor = jnp.exp2(highest - higher)
            slope = product(block(step, 1), do_cols[:, rows])
            weights[pl.ds(first, KEYS), :] = weight
            slopes[pl.ds(first, KEYS), :] = slope
            maxima[pl.ds(step * 8, 8), :] = jnp.broadcast_to(higher, (8, ROWS))
            norm = norm * factor + jnp.sum(weight, axis=0, keepdims=True)
            weighted = weighted * factor + jnp.sum(weight * slope, axis=0, keepdims=True)
            return higher, norm, weighted

        zeros = jnp.zeros((1, ROWS), F32)
        carry = lax.fori_loop(
            0, steps - 1, functools.partial(statistics, masked=False),
            (jnp.full((1, ROWS), -jnp.inf, F32), zeros, zeros),
        )
        highest, norm, weighted = statistics(steps - 1, carry, True)
        inverse = 1.0 / norm
        centre = weighted * inverse

        def gradients(step, dq_cols):
            keys = pl.ds(pl.multiple_of(step * KEYS, KEYS), KEYS)
            factor = jnp.exp2(maxima[pl.ds(step * 8, 8), :][0:1] - highest) * inverse
            soft = weights[keys, :] * factor
            score_grad = (soft * (slopes[keys, :] - centre)).astype(BF16)
            dk = product(score_grad, q_rows[rows, :])
            dv = product(soft.astype(BF16), do_rows[rows, :])
            if tile == 0:
                total[keys, 0:HEAD_SIZE] = dk
                total[keys, HEAD_SIZE:] = dv
            else:
                total[keys, 0:HEAD_SIZE] += dk
                total[keys, HEAD_SIZE:] += dv
            return dq_cols + product(k_cols[:, keys], score_grad)

        dq_cols = lax.fori_loop(0, steps, gradients, jnp.zeros((HEAD_SIZE, ROWS), F32)) * scale
        for i in range(ROWS // tokens):
            h = tile * (ROWS // tokens) + i
            dq_ref[:, h * HEAD_SIZE : (h + 1) * HEAD_SIZE] = dq_cols[:, i * tokens : (i + 1) * tokens].T

    @pl.loop(0, slabs * steps_per_slab)
    def _(step):
        slab = lax.div(step, jnp.int32(steps_per_slab))
        first = lax.rem(step, jnp.int32(steps_per_slab)) * per_step
        keys = pl.ds(pl.multiple_of(step * KEYS, KEYS), KEYS)
        there = pl.ds(first, per_step)

        @pl.when(step < steps)
        def _():
            dk = (total[keys, 0:HEAD_SIZE] * scale).astype(BF16)
            dv = total[keys, HEAD_SIZE:].astype(BF16)
            dkv_ref[there, slab, :, 0:HEAD_SIZE] = dk.reshape(per_step, tokens, HEAD_SIZE)
            dkv_ref[there, slab, :, HEAD_SIZE:] = dv.reshape(per_step, tokens, HEAD_SIZE)

        @pl.when(step >= steps)
        def _():
            dkv_ref[there, slab] = jnp.zeros((per_step, tokens, 2 * HEAD_SIZE), BF16)


def attention_gradients(rank, q, do, kv):
    tokens, width = q.shape
    rows = tokens * (width // HEAD_SIZE)
    keys = kv.shape[0] * kv.shape[1] * kv.shape[2]
    whole = pl.BlockSpec(memory_space=pltpu.VMEM)
    return pl.pallas_call(
        attention_kernel,
        out_shape=(jax.ShapeDtypeStruct(q.shape, F32), jax.ShapeDtypeStruct(kv.shape, BF16)),
        in_specs=[pl.BlockSpec(memory_space=pltpu.SMEM), whole, whole, whole],
        out_specs=(whole, whole),
        scratch_shapes=[
            pltpu.VMEM((rows, HEAD_SIZE), BF16),
            pltpu.VMEM((rows, HEAD_SIZE), BF16),
            pltpu.VMEM((HEAD_SIZE, rows), BF16),
            pltpu.VMEM((HEAD_SIZE, rows), BF16),
            pltpu.VMEM((HEAD_SIZE, keys), BF16),
            pltpu.VMEM((keys, ROWS), F32),
            pltpu.VMEM((keys, ROWS), F32),
            pltpu.VMEM((8 * keys // KEYS, ROWS), F32),
            pltpu.VMEM((keys, 2 * HEAD_SIZE), F32),
        ],
        compiler_params=pltpu.CompilerParams(vmem_limit_bytes=48 * 2**20),
        cost_estimate=pl.CostEstimate(
            flops=10 * rows * keys * HEAD_SIZE, bytes_accessed=6 * 2**20, transcendentals=rows * keys
        ),
        name="attention_gradients",
    )(rank, q, do, kv)


def slab_lists(ctx_count, tp_count):
    span = ctx_count // GROUPS
    plane = span // SLABS
    lists = []
    for t in range(tp_count):
        first = span // 2 if t >= tp_count // 2 else 0
        for g in range(GROUPS):
            for p in range(plane):
                column = [(first + g * span + s * plane + p) % ctx_count for s in range(SLABS)]
                lists.append([c * tp_count + t for c in column])
    return lists


def plane_lists(ctx_count, tp_count):
    plane = ctx_count // GROUPS // SLABS
    return [
        [(s * plane + p) * tp_count + t for p in range(plane)]
        for t in range(tp_count)
        for s in range(ctx_count // plane)
    ]


def exchange(parts, lists):
    return lax.all_to_all(parts, AXES, 0, 0, axis_index_groups=lists, tiled=True)


def shards(query_heads, key_heads_wide, value_heads_wide, grad_output):
    ctx_count = lax.axis_size("ctx")
    tp_count = lax.axis_size("tp")
    span = ctx_count // GROUPS
    plane = span // SLABS
    here = key_heads_wide.shape[0]
    rows = query_heads.shape[0]
    columns = slab_lists(ctx_count, tp_count)
    planes = plane_lists(ctx_count, tp_count)
    offset = jnp.where(lax.axis_index("tp") >= tp_count // 2, span // 2, 0)
    rank = jnp.mod(lax.axis_index("ctx") - offset, ctx_count) % span

    both = jnp.stack(
        [a.reshape(here, tp_count, HEAD_SIZE) for a in (key_heads_wide, value_heads_wide)], axis=2
    ).transpose(1, 0, 2, 3).reshape(tp_count, here, 2 * HEAD_SIZE)
    own = lax.all_to_all(both, "tp", 0, 0, tiled=True).reshape(rows, 2 * HEAD_SIZE)
    column = exchange(jnp.broadcast_to(own, (SLABS,) + own.shape), columns)
    kv = exchange(jnp.broadcast_to(column, (plane,) + column.shape), planes)
    grad_query, dkv = attention_gradients(rank.astype(jnp.int32).reshape(1), query_heads, grad_output, kv)
    partial = jnp.sum(exchange(dkv, planes).astype(F32), axis=0).astype(BF16)
    mine = jnp.sum(exchange(partial, columns).astype(F32), axis=0)
    back = lax.all_to_all(mine.reshape(tp_count, here, 2 * HEAD_SIZE), "tp", 0, 0, tiled=True)
    back = back.reshape(tp_count, here, 2, HEAD_SIZE).transpose(2, 1, 0, 3)
    back = back.reshape(2, here, tp_count * HEAD_SIZE)
    return grad_query, back[0], back[1]


def solution(mesh):
    return jax.shard_map(
        shards,
        mesh=mesh,
        in_specs=(P("ctx", "tp"), P(AXES, None), P(AXES, None), P("ctx", "tp")),
        out_specs=(P("ctx", "tp"), P(AXES, None), P(AXES, None)),
        check_vma=False,
    )
```

```python
import functools
import math

import jax
import jax.numpy as jnp
from jax import lax
from jax.experimental import pallas as pl
from jax.experimental.pallas import tpu as pltpu
from jax.sharding import PartitionSpec as P

HEAD_SIZE = 128
GROUPS = 4
SLABS = 4
PAIR = 2
ROWS = 512
LOWEST = -1e30
AXES = ("ctx", "tp")
BF16, F32 = jnp.bfloat16, jnp.float32
SCALE = 1.0 / math.sqrt(HEAD_SIZE)


def product(a, b):
    return jnp.dot(a, b, preferred_element_type=F32)


def keys_of(kv_ref, slab, column):
    part = kv_ref[:, slab, :, column * HEAD_SIZE : (column + 1) * HEAD_SIZE]
    return part.reshape(part.shape[0] * part.shape[1], HEAD_SIZE)


def statistics_kernel(
    place_ref, q_ref, do_ref, peer_ref, kv_ref, stats_ref, weights_ref, slopes_ref, q_cols, do_cols
):
    tokens, width = q_ref.shape
    heads = width // HEAD_SIZE
    mine = heads * tokens
    keys = kv_ref.shape[0] * kv_ref.shape[2]
    slab, along_y, along_x = place_ref[0], place_ref[1], place_ref[2]

    for owner in range(PAIR):
        q = q_ref if owner == 0 else peer_ref.at[0]
        do = do_ref if owner == 0 else peer_ref.at[1]
        for h in range(heads):
            across = slice(h * HEAD_SIZE, (h + 1) * HEAD_SIZE)
            down = slice(owner * mine + h * tokens, owner * mine + (h + 1) * tokens)
            q_cols[:, down] = q[:, across].T
            do_cols[:, down] = do[:, across].T

    for tile in range(PAIR * mine // ROWS):
        rows = slice(tile * ROWS, (tile + 1) * ROWS)

        def step(s, carry, masked):
            highest, norm, weighted = carry
            scores = product(keys_of(kv_ref, s, 0), q_cols[:, rows]) * (SCALE * math.log2(math.e))
            if masked:
                key = lax.broadcasted_iota(jnp.int32, (keys, ROWS), 0)
                if tile * ROWS < mine:
                    last = along_y * tokens + lax.rem(
                        lax.broadcasted_iota(jnp.int32, (keys, ROWS), 1), jnp.int32(tokens)
                    )
                else:
                    last = (along_y + 1 - along_x) * tokens - 1
                scores = jnp.where(key <= last, scores, LOWEST)
            higher = jnp.maximum(highest, jnp.max(scores, axis=0, keepdims=True))
            weight = jnp.exp2(scores - higher)
            factor = jnp.exp2(highest - higher)
            slope = product(keys_of(kv_ref, s, 1), do_cols[:, rows])
            weights_ref[s, :, rows] = weight.astype(weights_ref.dtype)
            slopes_ref[s, :, rows] = slope.astype(slopes_ref.dtype)
            stats_ref[pl.ds(s, 1), rows] = higher
            norm = norm * factor + jnp.sum(weight, axis=0, keepdims=True)
            weighted = weighted * factor + jnp.sum(weight * slope, axis=0, keepdims=True)
            return higher, norm, weighted

        zeros = jnp.zeros((1, ROWS), F32)
        carry = lax.fori_loop(
            0, slab, functools.partial(step, masked=False),
            (jnp.full((1, ROWS), LOWEST, F32), zeros, zeros),
        )
        highest, norm, weighted = step(slab, carry, True)
        stats_ref[SLABS : SLABS + 1, rows] = highest
        stats_ref[SLABS + 1 : SLABS + 2, rows] = norm
        stats_ref[SLABS + 2 : SLABS + 3, rows] = weighted


def gradients_kernel(
    place_ref, q_ref, do_ref, peer_ref, kv_ref, stats_ref, other_ref, weights_ref, slopes_ref,
    dq_ref, dq_peer_ref, dkv_ref,
    q_rows, do_rows, k_cols, total,
):
    tokens, width = q_ref.shape
    heads = width // HEAD_SIZE
    mine = heads * tokens
    along_y = kv_ref.shape[0]
    keys = along_y * tokens
    slab = place_ref[0]

    for owner in range(PAIR):
        q = q_ref if owner == 0 else peer_ref.at[0]
        do = do_ref if owner == 0 else peer_ref.at[1]
        for h in range(heads):
            across = slice(h * HEAD_SIZE, (h + 1) * HEAD_SIZE)
            down = slice(owner * mine + h * tokens, owner * mine + (h + 1) * tokens)
            q_rows[down, :] = q[:, across]
            do_rows[down, :] = do[:, across]

    @pl.loop(0, slab + 1)
    def _(s):
        k_cols[s] = keys_of(kv_ref, s, 0).T

    for tile in range(PAIR * mine // ROWS):
        rows = slice(tile * ROWS, (tile + 1) * ROWS)
        there = slice((tile * ROWS + mine) % (PAIR * mine), (tile * ROWS + mine) % (PAIR * mine) + ROWS)
        here_highest = stats_ref[SLABS : SLABS + 1, rows]
        there_highest = other_ref[SLABS : SLABS + 1, there]
        highest = jnp.maximum(here_highest, there_highest)
        here_factor = jnp.exp2(here_highest - highest)
        there_factor = jnp.exp2(there_highest - highest)

        def merged(i):
            at = slice(SLABS + i, SLABS + i + 1)
            return stats_ref[at, rows] * here_factor + other_ref[at, there] * there_factor

        inverse = 1.0 / merged(1)
        centre = merged(2) * inverse

        def step(s, dq_cols):
            factor = jnp.exp2(stats_ref[pl.ds(s, 1), rows] - highest) * inverse
            soft = weights_ref[s, :, rows].astype(F32) * factor
            score_grad = (soft * (slopes_ref[s, :, rows].astype(F32) - centre)).astype(BF16)
            dk = product(score_grad, q_rows[rows, :])
            dv = product(soft.astype(BF16), do_rows[rows, :])
            if tile == 0:
                total[s, :, 0:HEAD_SIZE] = dk
                total[s, :, HEAD_SIZE:] = dv
            else:
                total[s, :, 0:HEAD_SIZE] += dk
                total[s, :, HEAD_SIZE:] += dv
            return dq_cols + product(k_cols[s], score_grad)

        dq_cols = lax.fori_loop(0, slab + 1, step, jnp.zeros((HEAD_SIZE, ROWS), F32)) * SCALE
        for i in range(ROWS // tokens):
            h = tile * (ROWS // tokens) + i
            out = dq_ref if h < heads else dq_peer_ref
            across = slice(h % heads * HEAD_SIZE, (h % heads + 1) * HEAD_SIZE)
            out[:, across] = dq_cols[:, i * tokens : (i + 1) * tokens].T.astype(out.dtype)

    @pl.loop(0, SLABS)
    def _(s):
        @pl.when(s <= slab)
        def _():
            dk = (total[s, :, 0:HEAD_SIZE] * SCALE).astype(BF16)
            dv = total[s, :, HEAD_SIZE:].astype(BF16)
            dkv_ref[:, s, :, 0:HEAD_SIZE] = dk.reshape(along_y, tokens, HEAD_SIZE)
            dkv_ref[:, s, :, HEAD_SIZE:] = dv.reshape(along_y, tokens, HEAD_SIZE)

        @pl.when(s > slab)
        def _():
            dkv_ref[:, s] = jnp.zeros((along_y, tokens, 2 * HEAD_SIZE), BF16)


WHOLE = pl.BlockSpec(memory_space=pltpu.VMEM)
SCALARS = pl.BlockSpec(memory_space=pltpu.SMEM)


def row_statistics(place, q, do, peer, kv):
    tokens, width = q.shape
    rows = PAIR * tokens * (width // HEAD_SIZE)
    keys = kv.shape[0] * kv.shape[2]
    return pl.pallas_call(
        statistics_kernel,
        out_shape=(
            jax.ShapeDtypeStruct((8, rows), F32),
            jax.ShapeDtypeStruct((SLABS, keys, rows), F32),
            jax.ShapeDtypeStruct((SLABS, keys, rows), F32),
        ),
        in_specs=[SCALARS, WHOLE, WHOLE, WHOLE, WHOLE],
        out_specs=(WHOLE, WHOLE, WHOLE),
        scratch_shapes=[pltpu.VMEM((HEAD_SIZE, rows), BF16), pltpu.VMEM((HEAD_SIZE, rows), BF16)],
        compiler_params=pltpu.CompilerParams(vmem_limit_bytes=12 * 2**20),
        cost_estimate=pl.CostEstimate(
            flops=4 * rows * SLABS * keys * HEAD_SIZE, bytes_accessed=2 * 2**20, transcendentals=rows * SLABS * keys
        ),
        name="row_statistics",
    )(place, q, do, peer, kv)


def attention_gradients(place, q, do, peer, kv, stats, other, weights, slopes):
    tokens, width = q.shape
    rows = PAIR * tokens * (width // HEAD_SIZE)
    keys = kv.shape[0] * kv.shape[2]
    return pl.pallas_call(
        gradients_kernel,
        out_shape=(
            jax.ShapeDtypeStruct(q.shape, F32),
            jax.ShapeDtypeStruct(q.shape, BF16),
            jax.ShapeDtypeStruct(kv.shape, BF16),
        ),
        in_specs=[SCALARS] + [WHOLE] * 8,
        out_specs=(WHOLE, WHOLE, WHOLE),
        scratch_shapes=[
            pltpu.VMEM((rows, HEAD_SIZE), BF16),
            pltpu.VMEM((rows, HEAD_SIZE), BF16),
            pltpu.VMEM((SLABS, HEAD_SIZE, keys), BF16),
            pltpu.VMEM((SLABS, keys, 2 * HEAD_SIZE), F32),
        ],
        compiler_params=pltpu.CompilerParams(vmem_limit_bytes=12 * 2**20),
        cost_estimate=pl.CostEstimate(
            flops=6 * rows * SLABS * keys * HEAD_SIZE, bytes_accessed=4 * 2**20, transcendentals=rows
        ),
        name="attention_gradients",
    )(place, q, do, peer, kv, stats, other, weights, slopes)


def line_lists(ctx_count, tp_count, along_z):
    span = ctx_count // GROUPS
    plane = span // SLABS
    lists = []
    for t in range(tp_count):
        first = span // 2 if t >= tp_count // 2 and along_z else 0
        for g in range(GROUPS):
            if along_z:
                lines = [[first + g * span + s * plane + p for s in range(SLABS)] for p in range(plane)]
            else:
                lines = [
                    [g * span + s * plane + y * PAIR + x for y in range(plane // PAIR)]
                    for s in range(SLABS)
                    for x in range(PAIR)
                ]
            lists += [[c % ctx_count * tp_count + t for c in line] for line in lines]
    return lists


def exchange(parts, lists):
    return lax.all_to_all(parts, AXES, 0, 0, axis_index_groups=lists, tiled=True)


def to_peer(array):
    return lax.ppermute(array, "ctx", [(c, c ^ 1) for c in range(lax.axis_size("ctx"))])


def shards(query_heads, key_heads_wide, value_heads_wide, grad_output):
    ctx_count = lax.axis_size("ctx")
    tp_count = lax.axis_size("tp")
    span = ctx_count // GROUPS
    plane = span // SLABS
    lines = plane // PAIR
    here = key_heads_wide.shape[0]
    rows = query_heads.shape[0]
    along_z = line_lists(ctx_count, tp_count, True)
    along_y = line_lists(ctx_count, tp_count, False)
    offset = jnp.where(lax.axis_index("tp") >= tp_count // 2, span // 2, 0)
    rank = (jnp.mod(lax.axis_index("ctx") - offset, ctx_count) % span).astype(jnp.int32)
    place = jnp.stack([rank // plane, rank % plane // PAIR, rank % PAIR])

    peer = to_peer(jnp.stack([query_heads, grad_output]))
    both = jnp.stack(
        [a.reshape(here, tp_count, HEAD_SIZE) for a in (key_heads_wide, value_heads_wide)], axis=2
    ).transpose(1, 0, 2, 3).reshape(tp_count, here, 2 * HEAD_SIZE)
    own = lax.all_to_all(both, "tp", 0, 0, tiled=True).reshape(rows, 2 * HEAD_SIZE)
    column = exchange(jnp.broadcast_to(own, (SLABS,) + own.shape), along_z)
    kv = exchange(jnp.broadcast_to(column, (lines,) + column.shape), along_y)
    stats, weights, slopes = row_statistics(place, query_heads, grad_output, peer, kv)
    other = to_peer(stats)
    dq, dq_peer, dkv = attention_gradients(
        place, query_heads, grad_output, peer, kv, stats, other, weights, slopes
    )
    grad_query = dq + to_peer(dq_peer).astype(F32)
    partial = jnp.sum(exchange(dkv, along_y).astype(F32), axis=0).astype(BF16)
    mine = jnp.sum(exchange(partial, along_z).astype(F32), axis=0)
    back = lax.all_to_all(mine.reshape(tp_count, here, 2 * HEAD_SIZE), "tp", 0, 0, tiled=True)
    back = back.reshape(tp_count, here, 2, HEAD_SIZE).transpose(2, 1, 0, 3)
    back = back.reshape(2, here, tp_count * HEAD_SIZE)
    return grad_query, back[0], back[1]


def solution(mesh):
    return jax.shard_map(
        shards,
        mesh=mesh,
        in_specs=(P("ctx", "tp"), P(AXES, None), P(AXES, None), P("ctx", "tp")),
        out_specs=(P("ctx", "tp"), P(AXES, None), P(AXES, None)),
        check_vma=False,
    )
```

```python
import functools
import math

import jax
import jax.numpy as jnp
from jax import lax
from jax.experimental import pallas as pl
from jax.experimental.pallas import tpu as pltpu
from jax.sharding import PartitionSpec as P

HEAD_SIZE = 128
GROUPS = 4
SLABS = 4
PAIR = 2
ROWS = 1024
LOWEST = -1e30
AXES = ("ctx", "tp")
BF16, F32 = jnp.bfloat16, jnp.float32
SCALE = 1.0 / math.sqrt(HEAD_SIZE)


def product(a, b):
    return jnp.dot(a, b, preferred_element_type=F32)


def product_of_rows(a, b):
    return lax.dot_general(a, b, (((1,), (1,)), ((), ())), preferred_element_type=F32)


def keys_of(kv_ref, slab, column):
    part = kv_ref[:, slab, :, column * HEAD_SIZE : (column + 1) * HEAD_SIZE]
    return part.reshape(part.shape[0] * part.shape[1], HEAD_SIZE)


def by_head(ref, out):
    tokens = ref.shape[0]
    for h in range(ref.shape[1] // HEAD_SIZE):
        out[h * tokens : (h + 1) * tokens, :] = ref[:, h * HEAD_SIZE : (h + 1) * HEAD_SIZE]


def row_of(ref, i, tile):
    width = ref.shape[1]
    first = 8 * i + tile * (ROWS // width)
    return jnp.concatenate([ref[r : r + 1, :] for r in range(first, first + ROWS // width)], axis=1)


def rows_kernel(q_ref, do_ref, q_rows, do_rows):
    by_head(q_ref, q_rows)
    by_head(do_ref, do_rows)


def statistics_kernel(of_peer, place_ref, *refs):
    if of_peer:
        q_ref, do_ref, kv_ref, own_stats, stats_ref, maxima_ref, weights_ref, slopes_ref, q_rows, do_rows = refs
        rows_kernel(q_ref, do_ref, q_rows, do_rows)
        stats_ref[...] = own_stats[...]
    else:
        q_rows, do_rows, kv_ref, stats_ref, maxima_ref, weights_ref, slopes_ref = refs
    tokens = kv_ref.shape[2]
    keys = kv_ref.shape[0] * kv_ref.shape[2]
    slab, along_y, along_x = place_ref[0], place_ref[1], place_ref[2]

    def step(s, carry, masked):
        highest, norm, weighted = carry
        scores = product_of_rows(keys_of(kv_ref, s, 0), q_rows[...]) * (SCALE * math.log2(math.e))
        if masked:
            key = lax.broadcasted_iota(jnp.int32, (keys, ROWS), 0)
            if of_peer:
                last = (along_y + 1 - along_x) * tokens - 1
            else:
                token = lax.rem(lax.broadcasted_iota(jnp.int32, (keys, ROWS), 1), jnp.int32(tokens))
                last = along_y * tokens + token
            scores = jnp.where(key <= last, scores, LOWEST)
        higher = jnp.maximum(highest, jnp.max(scores, axis=0, keepdims=True))
        weight = jnp.exp2(scores - higher)
        factor = jnp.exp2(highest - higher)
        slope = product_of_rows(keys_of(kv_ref, s, 1), do_rows[...])
        weights_ref[s] = weight.astype(BF16)
        slopes_ref[s] = slope
        maxima_ref[pl.ds(s, 1), :] = higher
        norm = norm * factor + jnp.sum(weight, axis=0, keepdims=True)
        weighted = weighted * factor + jnp.sum(weight * slope, axis=0, keepdims=True)
        return higher, norm, weighted

    zeros = jnp.zeros((1, ROWS), F32)
    carry = lax.fori_loop(
        0, slab, functools.partial(step, masked=False), (jnp.full((1, ROWS), LOWEST, F32), zeros, zeros)
    )
    width = stats_ref.shape[1]
    for i, row in enumerate(step(slab, carry, True)):
        for j in range(ROWS // width):
            at = 8 * i + of_peer * (ROWS // width) + j
            stats_ref[at : at + 1, :] = row[:, j * width : (j + 1) * width]


def gradients_kernel(
    place_ref, own_q, own_do, peer_q, peer_do, kv_ref, stats_ref, other_ref,
    own_maxima, own_weights, own_slopes, peer_maxima, peer_weights, peer_slopes,
    dq_ref, dq_peer_ref, dkv_ref,
    there_q, there_do, k_cols, total,
):
    tokens, width = peer_q.shape
    heads = width // HEAD_SIZE
    along_y = kv_ref.shape[0]
    slab = place_ref[0]
    rows_kernel(peer_q, peer_do, there_q, there_do)

    @pl.loop(0, slab + 1)
    def _(s):
        k_cols[s] = keys_of(kv_ref, s, 0).T

    for owner in range(PAIR):
        q_rows, do_rows = (there_q, there_do) if owner else (own_q, own_do)
        maxima = peer_maxima if owner else own_maxima
        weights = peer_weights if owner else own_weights
        slopes = peer_slopes if owner else own_slopes
        here_highest, there_highest = row_of(stats_ref, 0, owner), row_of(other_ref, 0, 1 - owner)
        highest = jnp.maximum(here_highest, there_highest)
        here_factor, there_factor = jnp.exp2(here_highest - highest), jnp.exp2(there_highest - highest)
        inverse = 1.0 / (row_of(stats_ref, 1, owner) * here_factor + row_of(other_ref, 1, 1 - owner) * there_factor)
        centre = row_of(stats_ref, 2, owner) * here_factor + row_of(other_ref, 2, 1 - owner) * there_factor
        centre = centre * inverse

        def step(s, dq_cols):
            factor = jnp.exp2(maxima[pl.ds(s, 1), :] - highest) * inverse
            soft = weights[s].astype(F32) * factor
            score_grad = (soft * (slopes[s] - centre)).astype(BF16)
            dk = product(score_grad, q_rows[...])
            dv = product(soft.astype(BF16), do_rows[...])
            if owner == 0:
                total[s, :, 0:HEAD_SIZE] = dk
                total[s, :, HEAD_SIZE:] = dv
            else:
                total[s, :, 0:HEAD_SIZE] += dk
                total[s, :, HEAD_SIZE:] += dv
            return dq_cols + product(k_cols[s], score_grad)

        dq_cols = lax.fori_loop(0, slab + 1, step, jnp.zeros((HEAD_SIZE, ROWS), F32)) * SCALE
        out = dq_peer_ref if owner else dq_ref
        for h in range(heads):
            part = dq_cols[:, h * tokens : (h + 1) * tokens].T
            out[:, h * HEAD_SIZE : (h + 1) * HEAD_SIZE] = part.astype(out.dtype)

    @pl.loop(0, SLABS)
    def _(s):
        @pl.when(s <= slab)
        def _():
            dk = (total[s, :, 0:HEAD_SIZE] * SCALE).astype(BF16)
            dv = total[s, :, HEAD_SIZE:].astype(BF16)
            dkv_ref[:, s, :, 0:HEAD_SIZE] = dk.reshape(along_y, tokens, HEAD_SIZE)
            dkv_ref[:, s, :, HEAD_SIZE:] = dv.reshape(along_y, tokens, HEAD_SIZE)

        @pl.when(s > slab)
        def _():
            dkv_ref[:, s] = jnp.zeros((along_y, tokens, 2 * HEAD_SIZE), BF16)


def pack_kernel(key_ref, value_ref, out_ref):
    for h in range(out_ref.shape[0]):
        across = slice(h * HEAD_SIZE, (h + 1) * HEAD_SIZE)
        out_ref[h, :, 0:HEAD_SIZE] = key_ref[:, across]
        out_ref[h, :, HEAD_SIZE:] = value_ref[:, across]


def unpack_kernel(both_ref, key_ref, value_ref, sems):
    copies = [
        pltpu.make_async_copy(
            both_ref.at[h, :, i * HEAD_SIZE : (i + 1) * HEAD_SIZE],
            ref.at[:, h * HEAD_SIZE : (h + 1) * HEAD_SIZE],
            sems.at[i, h],
        )
        for i, ref in enumerate((key_ref, value_ref))
        for h in range(both_ref.shape[0])
    ]
    for copy in copies:
        copy.start()
    for copy in copies:
        copy.wait()


def sum_kernel(parts_ref, out_ref):
    total = parts_ref[0].astype(F32)
    for i in range(1, parts_ref.shape[0]):
        total += parts_ref[i].astype(F32)
    out_ref[...] = total.astype(out_ref.dtype)


WHOLE = pl.BlockSpec(memory_space=pltpu.VMEM)
IN_HBM = pl.BlockSpec(memory_space=pltpu.HBM)


def small(kernel, name, out, in_specs, out_specs, scratch, room, *args):
    moved = sum(a.size * a.dtype.itemsize for a in args)
    return pl.pallas_call(
        kernel,
        out_shape=out,
        in_specs=in_specs,
        out_specs=out_specs,
        scratch_shapes=scratch,
        compiler_params=pltpu.CompilerParams(vmem_limit_bytes=room * 2**20),
        cost_estimate=pl.CostEstimate(flops=0, bytes_accessed=2 * moved, transcendentals=0),
        name=name,
    )(*args)


def summed(parts, dtype):
    shape = jax.ShapeDtypeStruct(parts.shape[1:], dtype)
    return small(sum_kernel, "sum_of_parts", shape, [WHOLE], WHOLE, [], 4, parts)
SCALARS = pl.BlockSpec(memory_space=pltpu.SMEM)


def row_statistics(of_peer, place, q, do, kv, *own_stats):
    keys = kv.shape[0] * kv.shape[2]
    return pl.pallas_call(
        functools.partial(statistics_kernel, of_peer),
        out_shape=(
            jax.ShapeDtypeStruct((24, PAIR * ROWS // 8), F32),
            jax.ShapeDtypeStruct((8, ROWS), F32),
            jax.ShapeDtypeStruct((SLABS, keys, ROWS), BF16),
            jax.ShapeDtypeStruct((SLABS, keys, ROWS), F32),
        ),
        in_specs=[SCALARS] + [WHOLE] * (3 + len(own_stats)),
        out_specs=(WHOLE,) * 4,
        scratch_shapes=[pltpu.VMEM((ROWS, HEAD_SIZE), BF16)] * 2 if of_peer else [],
        compiler_params=pltpu.CompilerParams(vmem_limit_bytes=12 * 2**20),
        cost_estimate=pl.CostEstimate(
            flops=4 * ROWS * SLABS * keys * HEAD_SIZE, bytes_accessed=2**20, transcendentals=ROWS * SLABS * keys
        ),
        name="row_statistics",
    )(place, q, do, kv, *own_stats)


def attention_gradients(place, *args):
    q, kv = args[2], args[4]
    keys = kv.shape[0] * kv.shape[2]
    return pl.pallas_call(
        gradients_kernel,
        out_shape=(
            jax.ShapeDtypeStruct(q.shape, F32),
            jax.ShapeDtypeStruct(q.shape, BF16),
            jax.ShapeDtypeStruct(kv.shape, BF16),
        ),
        in_specs=[SCALARS] + [WHOLE] * len(args),
        out_specs=(WHOLE, WHOLE, WHOLE),
        scratch_shapes=[
            pltpu.VMEM((ROWS, HEAD_SIZE), BF16),
            pltpu.VMEM((ROWS, HEAD_SIZE), BF16),
            pltpu.VMEM((SLABS, HEAD_SIZE, keys), BF16),
            pltpu.VMEM((SLABS, keys, 2 * HEAD_SIZE), F32),
        ],
        compiler_params=pltpu.CompilerParams(vmem_limit_bytes=18 * 2**20),
        cost_estimate=pl.CostEstimate(
            flops=12 * ROWS * SLABS * keys * HEAD_SIZE, bytes_accessed=4 * 2**20, transcendentals=ROWS
        ),
        name="attention_gradients",
    )(place, *args)


def line_lists(ctx_count, tp_count, along_z):
    span = ctx_count // GROUPS
    plane = span // SLABS
    lists = []
    for t in range(tp_count):
        first = span // 2 if t >= tp_count // 2 and along_z else 0
        for g in range(GROUPS):
            if along_z:
                lines = [[first + g * span + s * plane + p for s in range(SLABS)] for p in range(plane)]
            else:
                lines = [
                    [g * span + s * plane + y * PAIR + x for y in range(plane // PAIR)]
                    for s in range(SLABS)
                    for x in range(PAIR)
                ]
            lists += [[c % ctx_count * tp_count + t for c in line] for line in lines]
    return lists


def exchange(parts, lists):
    return lax.all_to_all(parts, AXES, 0, 0, axis_index_groups=lists, tiled=True)


def to_peer(array):
    return lax.ppermute(array, "ctx", [(c, c ^ 1) for c in range(lax.axis_size("ctx"))])


def shards(query_heads, key_heads_wide, value_heads_wide, grad_output):
    ctx_count = lax.axis_size("ctx")
    tp_count = lax.axis_size("tp")
    span = ctx_count // GROUPS
    plane = span // SLABS
    lines = plane // PAIR
    here = key_heads_wide.shape[0]
    rows = query_heads.shape[0]
    along_z = line_lists(ctx_count, tp_count, True)
    along_y = line_lists(ctx_count, tp_count, False)
    offset = jnp.where(lax.axis_index("tp") >= tp_count // 2, span // 2, 0)
    rank = (jnp.mod(lax.axis_index("ctx") - offset, ctx_count) % span).astype(jnp.int32)
    place = jnp.stack([rank // plane, rank % plane // PAIR, rank % PAIR])

    peer_q, peer_do = to_peer(query_heads), to_peer(grad_output)
    shape = jax.ShapeDtypeStruct((ROWS, HEAD_SIZE), BF16)
    own_q, own_do = small(
        rows_kernel, "queries_by_head", (shape, shape), [WHOLE] * 2, (WHOLE, WHOLE), [], 4, query_heads, grad_output
    )
    both = small(
        pack_kernel, "keys_and_values_by_head", jax.ShapeDtypeStruct((tp_count, here, 2 * HEAD_SIZE), BF16),
        [WHOLE, WHOLE], WHOLE, [], 4, key_heads_wide, value_heads_wide,
    )
    own = lax.all_to_all(both, "tp", 0, 0, tiled=True).reshape(rows, 2 * HEAD_SIZE)
    column = exchange(jnp.broadcast_to(own, (SLABS,) + own.shape), along_z)
    kv = exchange(jnp.broadcast_to(column, (lines,) + column.shape), along_y)
    own_stats, *own_held = row_statistics(False, place, own_q, own_do, kv)
    stats, *peer_held = row_statistics(True, place, peer_q, peer_do, kv, own_stats)
    dq, dq_peer, dkv = attention_gradients(
        place, own_q, own_do, peer_q, peer_do, kv, stats, to_peer(stats), *own_held, *peer_held
    )
    grad_query = dq + to_peer(dq_peer).astype(F32)
    partial = summed(exchange(dkv, along_y), BF16)
    mine = summed(exchange(partial, along_z), F32)
    back = lax.all_to_all(mine.reshape(tp_count, here, 2 * HEAD_SIZE), "tp", 0, 0, tiled=True)
    shape = jax.ShapeDtypeStruct(key_heads_wide.shape, F32)
    key_gradient, value_gradient = small(
        unpack_kernel, "gradients_by_token", (shape, shape), [WHOLE], (IN_HBM, IN_HBM),
        [pltpu.SemaphoreType.DMA((2, tp_count))], 4, back
    )
    return grad_query, key_gradient, value_gradient


def solution(mesh):
    return jax.shard_map(
        shards,
        mesh=mesh,
        in_specs=(P("ctx", "tp"), P(AXES, None), P(AXES, None), P("ctx", "tp")),
        out_specs=(P("ctx", "tp"), P(AXES, None), P(AXES, None)),
        check_vma=False,
    )
```

```python
import functools
import math

import jax
import jax.numpy as jnp
from jax import lax
from jax.experimental import pallas as pl
from jax.experimental.pallas import tpu as pltpu
from jax.sharding import PartitionSpec as P

HEAD_SIZE = 128
GROUPS = 4
SLABS = 4
PAIR = 2
ROWS = 1024
LOWEST = -1e30
AXES = ("ctx", "tp")
BF16, F32 = jnp.bfloat16, jnp.float32
SCALE = 1.0 / math.sqrt(HEAD_SIZE)


def product(a, b):
    return jnp.dot(a, b, preferred_element_type=F32)


def product_of_rows(a, b):
    return lax.dot_general(a, b, (((1,), (1,)), ((), ())), preferred_element_type=F32)


def keys_of(kv_ref, slab, column):
    part = kv_ref[:, slab, :, column * HEAD_SIZE : (column + 1) * HEAD_SIZE]
    return part.reshape(part.shape[0] * part.shape[1], HEAD_SIZE)


def by_head(ref, out):
    tokens = ref.shape[0]
    for h in range(ref.shape[1] // HEAD_SIZE):
        out[h * tokens : (h + 1) * tokens, :] = ref[:, h * HEAD_SIZE : (h + 1) * HEAD_SIZE]


def row_of(ref, i, tile):
    width = ref.shape[1]
    first = 8 * i + tile * (ROWS // width)
    return jnp.concatenate([ref[r : r + 1, :] for r in range(first, first + ROWS // width)], axis=1)


def rows_kernel(q_ref, do_ref, q_rows, do_rows):
    by_head(q_ref, q_rows)
    by_head(do_ref, do_rows)


def statistics_kernel(of_peer, place_ref, *refs):
    if of_peer:
        q_ref, do_ref, kv_ref, own_stats, stats_ref, maxima_ref, weights_ref, slopes_ref, q_rows, do_rows = refs
        rows_kernel(q_ref, do_ref, q_rows, do_rows)
        stats_ref[...] = own_stats[...]
    else:
        q_rows, do_rows, kv_ref, stats_ref, maxima_ref, weights_ref, slopes_ref = refs
    tokens = kv_ref.shape[2]
    keys = kv_ref.shape[0] * kv_ref.shape[2]
    slab, along_y, along_x = place_ref[0], place_ref[1], place_ref[2]

    def step(s, carry, masked):
        highest, norm, weighted = carry
        scores = product_of_rows(keys_of(kv_ref, s, 0), q_rows[...]) * (SCALE * math.log2(math.e))
        if masked:
            key = lax.broadcasted_iota(jnp.int32, (keys, ROWS), 0)
            if of_peer:
                last = (along_y + 1 - along_x) * tokens - 1
            else:
                token = lax.rem(lax.broadcasted_iota(jnp.int32, (keys, ROWS), 1), jnp.int32(tokens))
                last = along_y * tokens + token
            scores = jnp.where(key <= last, scores, LOWEST)
        higher = jnp.maximum(highest, jnp.max(scores, axis=0, keepdims=True))
        weight = jnp.exp2(scores - higher)
        factor = jnp.exp2(highest - higher)
        slope = product_of_rows(keys_of(kv_ref, s, 1), do_rows[...])
        weights_ref[s] = weight.astype(BF16)
        slopes_ref[s] = slope
        maxima_ref[pl.ds(s, 1), :] = higher
        norm = norm * factor + jnp.sum(weight, axis=0, keepdims=True)
        weighted = weighted * factor + jnp.sum(weight * slope, axis=0, keepdims=True)
        return higher, norm, weighted

    def finish(carry):
        width = stats_ref.shape[1]
        for i, row in enumerate(step(slab, carry, True)):
            for j in range(ROWS // width):
                at = 8 * i + of_peer * (ROWS // width) + j
                stats_ref[at : at + 1, :] = row[:, j * width : (j + 1) * width]

    zeros = jnp.zeros((1, ROWS), F32)
    start = (jnp.full((1, ROWS), LOWEST, F32), zeros, zeros)

    @pl.when(slab == SLABS - 1)
    def _():
        carry = start
        for s in range(SLABS - 1):
            carry = step(s, carry, False)
        finish(carry)

    @pl.when(slab < SLABS - 1)
    def _():
        finish(lax.fori_loop(0, slab, functools.partial(step, masked=False), start))


def gradients_kernel(
    place_ref, own_q, own_do, peer_q, peer_do, kv_ref, stats_ref, other_ref,
    own_maxima, own_weights, own_slopes, peer_maxima, peer_weights, peer_slopes,
    dq_ref, dq_peer_ref, dkv_ref,
    there_q, there_do,
):
    tokens, width = peer_q.shape
    heads = width // HEAD_SIZE
    along_y = kv_ref.shape[0]
    slab = place_ref[0]
    rows_kernel(peer_q, peer_do, there_q, there_do)

    rows = ((own_q, own_do), (there_q, there_do))
    held = ((own_maxima, own_weights, own_slopes), (peer_maxima, peer_weights, peer_slopes))
    norms = []
    for owner in range(PAIR):
        here_highest, there_highest = row_of(stats_ref, 0, owner), row_of(other_ref, 0, 1 - owner)
        highest = jnp.maximum(here_highest, there_highest)
        here_factor, there_factor = jnp.exp2(here_highest - highest), jnp.exp2(there_highest - highest)
        inverse = 1.0 / (row_of(stats_ref, 1, owner) * here_factor + row_of(other_ref, 1, 1 - owner) * there_factor)
        centre = row_of(stats_ref, 2, owner) * here_factor + row_of(other_ref, 2, 1 - owner) * there_factor
        norms.append((highest, inverse, centre * inverse))

    def step(s, dq_cols):
        k_cols = keys_of(kv_ref, s, 0).T
        dk = dv = 0.0
        added = []
        for owner in range(PAIR):
            (q_rows, do_rows), (maxima, weights, slopes) = rows[owner], held[owner]
            highest, inverse, centre = norms[owner]
            factor = jnp.exp2(maxima[pl.ds(s, 1), :] - highest) * inverse
            soft = weights[s].astype(F32) * factor
            score_grad = (soft * (slopes[s] - centre)).astype(BF16)
            dk += product(score_grad, q_rows[...])
            dv += product(soft.astype(BF16), do_rows[...])
            added.append(dq_cols[owner] + product(k_cols, score_grad))
        dkv_ref[:, s, :, 0:HEAD_SIZE] = (dk * SCALE).astype(BF16).reshape(along_y, tokens, HEAD_SIZE)
        dkv_ref[:, s, :, HEAD_SIZE:] = dv.astype(BF16).reshape(along_y, tokens, HEAD_SIZE)
        return tuple(added)

    def finish(dq_cols):
        for cols, out in zip(dq_cols, (dq_ref, dq_peer_ref)):
            for h in range(heads):
                part = cols[:, h * tokens : (h + 1) * tokens].T * SCALE
                out[:, h * HEAD_SIZE : (h + 1) * HEAD_SIZE] = part.astype(out.dtype)

    start = (jnp.zeros((HEAD_SIZE, ROWS), F32),) * PAIR

    @pl.when(slab == SLABS - 1)
    def _():
        dq_cols = start
        for s in range(SLABS):
            dq_cols = step(s, dq_cols)
        finish(dq_cols)

    @pl.when(slab < SLABS - 1)
    def _():
        finish(lax.fori_loop(0, slab + 1, step, start))

        @pl.loop(slab + 1, SLABS)
        def _(s):
            dkv_ref[:, s] = jnp.zeros((along_y, tokens, 2 * HEAD_SIZE), BF16)


def pack_kernel(key_ref, value_ref, out_ref):
    for h in range(out_ref.shape[0]):
        across = slice(h * HEAD_SIZE, (h + 1) * HEAD_SIZE)
        out_ref[h, :, 0:HEAD_SIZE] = key_ref[:, across]
        out_ref[h, :, HEAD_SIZE:] = value_ref[:, across]


def unpack_kernel(both_ref, key_ref, value_ref, sems):
    copies = [
        pltpu.make_async_copy(
            both_ref.at[h, :, i * HEAD_SIZE : (i + 1) * HEAD_SIZE],
            ref.at[:, h * HEAD_SIZE : (h + 1) * HEAD_SIZE],
            sems.at[i, h],
        )
        for i, ref in enumerate((key_ref, value_ref))
        for h in range(both_ref.shape[0])
    ]
    for copy in copies:
        copy.start()
    for copy in copies:
        copy.wait()


def sum_kernel(parts_ref, out_ref):
    total = parts_ref[0].astype(F32)
    for i in range(1, parts_ref.shape[0]):
        total += parts_ref[i].astype(F32)
    out_ref[...] = total.astype(out_ref.dtype)


WHOLE = pl.BlockSpec(memory_space=pltpu.VMEM)
IN_HBM = pl.BlockSpec(memory_space=pltpu.HBM)


def small(kernel, name, out, in_specs, out_specs, scratch, room, *args):
    moved = sum(a.size * a.dtype.itemsize for a in args)
    return pl.pallas_call(
        kernel,
        out_shape=out,
        in_specs=in_specs,
        out_specs=out_specs,
        scratch_shapes=scratch,
        compiler_params=pltpu.CompilerParams(vmem_limit_bytes=room * 2**20),
        cost_estimate=pl.CostEstimate(flops=0, bytes_accessed=2 * moved, transcendentals=0),
        name=name,
    )(*args)


def summed(parts, dtype):
    shape = jax.ShapeDtypeStruct(parts.shape[1:], dtype)
    return small(sum_kernel, "sum_of_parts", shape, [WHOLE], WHOLE, [], 4, parts)
SCALARS = pl.BlockSpec(memory_space=pltpu.SMEM)


def row_statistics(of_peer, place, q, do, kv, *own_stats):
    keys = kv.shape[0] * kv.shape[2]
    return pl.pallas_call(
        functools.partial(statistics_kernel, of_peer),
        out_shape=(
            jax.ShapeDtypeStruct((24, PAIR * ROWS // 8), F32),
            jax.ShapeDtypeStruct((8, ROWS), F32),
            jax.ShapeDtypeStruct((SLABS, keys, ROWS), BF16),
            jax.ShapeDtypeStruct((SLABS, keys, ROWS), F32),
        ),
        in_specs=[SCALARS] + [WHOLE] * (3 + len(own_stats)),
        out_specs=(WHOLE,) * 4,
        scratch_shapes=[pltpu.VMEM((ROWS, HEAD_SIZE), BF16)] * 2 if of_peer else [],
        compiler_params=pltpu.CompilerParams(vmem_limit_bytes=12 * 2**20),
        cost_estimate=pl.CostEstimate(
            flops=4 * ROWS * SLABS * keys * HEAD_SIZE, bytes_accessed=2**20, transcendentals=ROWS * SLABS * keys
        ),
        name="row_statistics",
    )(place, q, do, kv, *own_stats)


def attention_gradients(place, *args):
    q, kv = args[2], args[4]
    keys = kv.shape[0] * kv.shape[2]
    return pl.pallas_call(
        gradients_kernel,
        out_shape=(
            jax.ShapeDtypeStruct(q.shape, F32),
            jax.ShapeDtypeStruct(q.shape, BF16),
            jax.ShapeDtypeStruct(kv.shape, BF16),
        ),
        in_specs=[SCALARS] + [WHOLE] * len(args),
        out_specs=(WHOLE, WHOLE, WHOLE),
        scratch_shapes=[
            pltpu.VMEM((ROWS, HEAD_SIZE), BF16),
            pltpu.VMEM((ROWS, HEAD_SIZE), BF16),
        ],
        compiler_params=pltpu.CompilerParams(vmem_limit_bytes=18 * 2**20),
        cost_estimate=pl.CostEstimate(
            flops=12 * ROWS * SLABS * keys * HEAD_SIZE, bytes_accessed=4 * 2**20, transcendentals=ROWS
        ),
        name="attention_gradients",
    )(place, *args)


def line_lists(ctx_count, tp_count, along_z):
    span = ctx_count // GROUPS
    plane = span // SLABS
    lists = []
    for t in range(tp_count):
        first = span // 2 if t >= tp_count // 2 and along_z else 0
        for g in range(GROUPS):
            if along_z:
                lines = [[first + g * span + s * plane + p for s in range(SLABS)] for p in range(plane)]
            else:
                lines = [
                    [g * span + s * plane + y * PAIR + x for y in range(plane // PAIR)]
                    for s in range(SLABS)
                    for x in range(PAIR)
                ]
            lists += [[c % ctx_count * tp_count + t for c in line] for line in lines]
    return lists


def exchange(parts, lists):
    return lax.all_to_all(parts, AXES, 0, 0, axis_index_groups=lists, tiled=True)


def to_peer(array):
    return lax.ppermute(array, "ctx", [(c, c ^ 1) for c in range(lax.axis_size("ctx"))])


def shards(query_heads, key_heads_wide, value_heads_wide, grad_output):
    ctx_count = lax.axis_size("ctx")
    tp_count = lax.axis_size("tp")
    span = ctx_count // GROUPS
    plane = span // SLABS
    lines = plane // PAIR
    here = key_heads_wide.shape[0]
    rows = query_heads.shape[0]
    along_z = line_lists(ctx_count, tp_count, True)
    along_y = line_lists(ctx_count, tp_count, False)
    offset = jnp.where(lax.axis_index("tp") >= tp_count // 2, span // 2, 0)
    rank = (jnp.mod(lax.axis_index("ctx") - offset, ctx_count) % span).astype(jnp.int32)
    place = jnp.stack([rank // plane, rank % plane // PAIR, rank % PAIR])

    peer_q, peer_do = to_peer(query_heads), to_peer(grad_output)
    shape = jax.ShapeDtypeStruct((ROWS, HEAD_SIZE), BF16)
    own_q, own_do = small(
        rows_kernel, "queries_by_head", (shape, shape), [WHOLE] * 2, (WHOLE, WHOLE), [], 4, query_heads, grad_output
    )
    both = small(
        pack_kernel, "keys_and_values_by_head", jax.ShapeDtypeStruct((tp_count, here, 2 * HEAD_SIZE), BF16),
        [WHOLE, WHOLE], WHOLE, [], 4, key_heads_wide, value_heads_wide,
    )
    own = lax.all_to_all(both, "tp", 0, 0, tiled=True).reshape(rows, 2 * HEAD_SIZE)
    column = exchange(jnp.broadcast_to(own, (SLABS,) + own.shape), along_z)
    kv = exchange(jnp.broadcast_to(column, (lines,) + column.shape), along_y)
    own_stats, *own_held = row_statistics(False, place, own_q, own_do, kv)
    stats, *peer_held = row_statistics(True, place, peer_q, peer_do, kv, own_stats)
    dq, dq_peer, dkv = attention_gradients(
        place, own_q, own_do, peer_q, peer_do, kv, stats, to_peer(stats), *own_held, *peer_held
    )
    grad_query = dq + to_peer(dq_peer).astype(F32)
    partial = summed(exchange(dkv, along_y), BF16)
    mine = summed(exchange(partial, along_z), F32)
    back = lax.all_to_all(mine.reshape(tp_count, here, 2 * HEAD_SIZE), "tp", 0, 0, tiled=True)
    shape = jax.ShapeDtypeStruct(key_heads_wide.shape, F32)
    key_gradient, value_gradient = small(
        unpack_kernel, "gradients_by_token", (shape, shape), [WHOLE], (IN_HBM, IN_HBM),
        [pltpu.SemaphoreType.DMA((2, tp_count))], 4, back
    )
    return grad_query, key_gradient, value_gradient


def solution(mesh):
    return jax.shard_map(
        shards,
        mesh=mesh,
        in_specs=(P("ctx", "tp"), P(AXES, None), P(AXES, None), P("ctx", "tp")),
        out_specs=(P("ctx", "tp"), P(AXES, None), P(AXES, None)),
        check_vma=False,
    )
```

```python
import functools
import math

import jax
import jax.numpy as jnp
from jax import lax
from jax.experimental import pallas as pl
from jax.experimental.pallas import tpu as pltpu
from jax.sharding import PartitionSpec as P

HEAD_SIZE = 128
GROUPS = 4
SLABS = 4
PAIR = 2
ROWS = 1024
LOWEST = -1e30
AXES = ("ctx", "tp")
BF16, F32 = jnp.bfloat16, jnp.float32
SCALE = 1.0 / math.sqrt(HEAD_SIZE)


def product(a, b):
    return jnp.dot(a, b, preferred_element_type=F32)


def product_of_rows(a, b):
    return lax.dot_general(a, b, (((1,), (1,)), ((), ())), preferred_element_type=F32)


def keys_of(kv_ref, slab, column):
    part = kv_ref[:, slab, :, column * HEAD_SIZE : (column + 1) * HEAD_SIZE]
    return part.reshape(part.shape[0] * part.shape[1], HEAD_SIZE)


def by_head(ref, out):
    tokens = ref.shape[0]
    for h in range(ref.shape[1] // HEAD_SIZE):
        out[h * tokens : (h + 1) * tokens, :] = ref[:, h * HEAD_SIZE : (h + 1) * HEAD_SIZE]


def row_of(ref, i, tile):
    width = ref.shape[1]
    first = 8 * i + tile * (ROWS // width)
    return jnp.concatenate([ref[r : r + 1, :] for r in range(first, first + ROWS // width)], axis=1)


def rows_kernel(q_ref, do_ref, q_rows, do_rows):
    by_head(q_ref, q_rows)
    by_head(do_ref, do_rows)


def statistics_kernel(of_peer, place_ref, *refs):
    if of_peer:
        q_ref, do_ref, kv_ref, own_stats, stats_ref, maxima_ref, weights_ref, slopes_ref, q_rows, do_rows = refs
        rows_kernel(q_ref, do_ref, q_rows, do_rows)
        stats_ref[...] = own_stats[...]
    else:
        q_rows, do_rows, kv_ref, stats_ref, maxima_ref, weights_ref, slopes_ref = refs
    tokens = kv_ref.shape[2]
    keys = kv_ref.shape[0] * kv_ref.shape[2]
    slab, along_y, along_x = place_ref[0], place_ref[1], place_ref[2]

    def step(s, carry, masked):
        highest, norm, weighted = carry
        scores = product_of_rows(keys_of(kv_ref, s, 0), q_rows[...]) * (SCALE * math.log2(math.e))
        if masked:
            key = lax.broadcasted_iota(jnp.int32, (keys, ROWS), 0)
            if of_peer:
                last = (along_y + 1 - along_x) * tokens - 1
            else:
                token = lax.rem(lax.broadcasted_iota(jnp.int32, (keys, ROWS), 1), jnp.int32(tokens))
                last = along_y * tokens + token
            scores = jnp.where(key <= last, scores, LOWEST)
        higher = jnp.maximum(highest, jnp.max(scores, axis=0, keepdims=True))
        weight = jnp.exp2(scores - higher)
        factor = jnp.exp2(highest - higher)
        slope = product_of_rows(keys_of(kv_ref, s, 1), do_rows[...])
        weights_ref[s] = weight.astype(BF16)
        slopes_ref[s] = slope
        maxima_ref[pl.ds(s, 1), :] = higher
        norm = norm * factor + jnp.sum(weight, axis=0, keepdims=True)
        weighted = weighted * factor + jnp.sum(weight * slope, axis=0, keepdims=True)
        return higher, norm, weighted

    def finish(carry):
        width = stats_ref.shape[1]
        for i, row in enumerate(step(slab, carry, True)):
            for j in range(ROWS // width):
                at = 8 * i + of_peer * (ROWS // width) + j
                stats_ref[at : at + 1, :] = row[:, j * width : (j + 1) * width]

    zeros = jnp.zeros((1, ROWS), F32)
    start = (jnp.full((1, ROWS), LOWEST, F32), zeros, zeros)

    @pl.when(slab == SLABS - 1)
    def _():
        carry = start
        for s in range(SLABS - 1):
            carry = step(s, carry, False)
        finish(carry)

    @pl.when(slab < SLABS - 1)
    def _():
        finish(lax.fori_loop(0, slab, functools.partial(step, masked=False), start))


def key_columns_kernel(kv_ref, k_cols):
    for s in range(SLABS):
        k_cols[s] = keys_of(kv_ref, s, 0).T


def query_rows_kernel(cols_ref, dq_ref, dq_peer_ref):
    tokens = dq_ref.shape[0]
    for owner, out in enumerate((dq_ref, dq_peer_ref)):
        for h in range(dq_ref.shape[1] // HEAD_SIZE):
            part = cols_ref[owner, :, h * tokens : (h + 1) * tokens].T
            out[:, h * HEAD_SIZE : (h + 1) * HEAD_SIZE] = part.astype(out.dtype)


def gradients_kernel(
    place_ref, own_q, own_do, peer_q, peer_do, kv_ref, stats_ref, other_ref,
    own_maxima, own_weights, own_slopes, peer_maxima, peer_weights, peer_slopes,
    k_cols, dq_ref, dkv_ref,
    there_q, there_do,
):
    tokens = peer_q.shape[0]
    along_y = kv_ref.shape[0]
    slab = place_ref[0]
    rows_kernel(peer_q, peer_do, there_q, there_do)

    rows = ((own_q, own_do), (there_q, there_do))
    held = ((own_maxima, own_weights, own_slopes), (peer_maxima, peer_weights, peer_slopes))
    norms = []
    for owner in range(PAIR):
        here_highest, there_highest = row_of(stats_ref, 0, owner), row_of(other_ref, 0, 1 - owner)
        highest = jnp.maximum(here_highest, there_highest)
        here_factor, there_factor = jnp.exp2(here_highest - highest), jnp.exp2(there_highest - highest)
        inverse = 1.0 / (row_of(stats_ref, 1, owner) * here_factor + row_of(other_ref, 1, 1 - owner) * there_factor)
        centre = row_of(stats_ref, 2, owner) * here_factor + row_of(other_ref, 2, 1 - owner) * there_factor
        norms.append((highest, inverse, centre * inverse))

    def step(s, dq_cols):
        dk = dv = 0.0
        added = []
        for owner in range(PAIR):
            (q_rows, do_rows), (maxima, weights, slopes) = rows[owner], held[owner]
            highest, inverse, centre = norms[owner]
            factor = jnp.exp2(maxima[pl.ds(s, 1), :] - highest) * inverse
            soft = weights[s].astype(F32) * factor
            score_grad = (soft * (slopes[s] - centre)).astype(BF16)
            dk += product(score_grad, q_rows[...])
            dv += product(soft.astype(BF16), do_rows[...])
            added.append(dq_cols[owner] + product(k_cols[s], score_grad))
        dkv_ref[:, s, :, 0:HEAD_SIZE] = (dk * SCALE).astype(BF16).reshape(along_y, tokens, HEAD_SIZE)
        dkv_ref[:, s, :, HEAD_SIZE:] = dv.astype(BF16).reshape(along_y, tokens, HEAD_SIZE)
        return tuple(added)

    def finish(dq_cols):
        for owner in range(PAIR):
            dq_ref[owner] = dq_cols[owner] * SCALE

    start = (jnp.zeros((HEAD_SIZE, ROWS), F32),) * PAIR

    @pl.when(slab == SLABS - 1)
    def _():
        dq_cols = start
        for s in range(SLABS):
            dq_cols = step(s, dq_cols)
        finish(dq_cols)

    @pl.when(slab < SLABS - 1)
    def _():
        finish(lax.fori_loop(0, slab + 1, step, start))

        @pl.loop(slab + 1, SLABS)
        def _(s):
            dkv_ref[:, s] = jnp.zeros((along_y, tokens, 2 * HEAD_SIZE), BF16)


def pack_kernel(both_ref, out_ref):
    for h in range(out_ref.shape[0]):
        for i in range(2):
            out_ref[h, :, i * HEAD_SIZE : (i + 1) * HEAD_SIZE] = both_ref[i, :, h * HEAD_SIZE : (h + 1) * HEAD_SIZE]


def finish_kernel(both_ref, dq_ref, peer_ref, key_ref, value_ref, query_ref, total, sems):
    heads = both_ref.shape[0]
    copies = [
        pltpu.make_async_copy(
            both_ref.at[h, :, i * HEAD_SIZE : (i + 1) * HEAD_SIZE],
            ref.at[:, h * HEAD_SIZE : (h + 1) * HEAD_SIZE],
            sems.at[i, h],
        )
        for i, ref in enumerate((key_ref, value_ref))
        for h in range(heads)
    ]
    for copy in copies:
        copy.start()
    tokens = total.shape[0] // heads
    for h in range(heads):
        down = slice(h * tokens, (h + 1) * tokens)
        total[down, :] = dq_ref[down, :] + peer_ref[down, :].astype(F32)
        copies.append(pltpu.make_async_copy(total.at[down, :], query_ref.at[down, :], sems.at[2, h]))
        copies[-1].start()
    for copy in copies:
        copy.wait()


def sum_kernel(parts_ref, out_ref):
    total = parts_ref[0].astype(F32)
    for i in range(1, parts_ref.shape[0]):
        total += parts_ref[i].astype(F32)
    out_ref[...] = total.astype(out_ref.dtype)


WHOLE = pl.BlockSpec(memory_space=pltpu.VMEM)
IN_HBM = pl.BlockSpec(memory_space=pltpu.HBM)


def small(kernel, name, out, in_specs, out_specs, scratch, room, *args):
    moved = sum(a.size * a.dtype.itemsize for a in args)
    return pl.pallas_call(
        kernel,
        out_shape=out,
        in_specs=in_specs,
        out_specs=out_specs,
        scratch_shapes=scratch,
        compiler_params=pltpu.CompilerParams(vmem_limit_bytes=room * 2**20),
        cost_estimate=pl.CostEstimate(flops=0, bytes_accessed=2 * moved, transcendentals=0),
        name=name,
    )(*args)


def summed(parts, dtype):
    shape = jax.ShapeDtypeStruct(parts.shape[1:], dtype)
    return small(sum_kernel, "sum_of_parts", shape, [WHOLE], WHOLE, [], 4, parts)
SCALARS = pl.BlockSpec(memory_space=pltpu.SMEM)


def row_statistics(of_peer, place, q, do, kv, *own_stats):
    keys = kv.shape[0] * kv.shape[2]
    return pl.pallas_call(
        functools.partial(statistics_kernel, of_peer),
        out_shape=(
            jax.ShapeDtypeStruct((24, PAIR * ROWS // 8), F32),
            jax.ShapeDtypeStruct((8, ROWS), F32),
            jax.ShapeDtypeStruct((SLABS, keys, ROWS), BF16),
            jax.ShapeDtypeStruct((SLABS, keys, ROWS), F32),
        ),
        in_specs=[SCALARS] + [WHOLE] * (3 + len(own_stats)),
        out_specs=(WHOLE,) * 4,
        scratch_shapes=[pltpu.VMEM((ROWS, HEAD_SIZE), BF16)] * 2 if of_peer else [],
        compiler_params=pltpu.CompilerParams(vmem_limit_bytes=12 * 2**20),
        cost_estimate=pl.CostEstimate(
            flops=4 * ROWS * SLABS * keys * HEAD_SIZE, bytes_accessed=2**20, transcendentals=ROWS * SLABS * keys
        ),
        name="row_statistics",
    )(place, q, do, kv, *own_stats)


def attention_gradients(place, *args):
    kv = args[4]
    keys = kv.shape[0] * kv.shape[2]
    return pl.pallas_call(
        gradients_kernel,
        out_shape=(
            jax.ShapeDtypeStruct((PAIR, HEAD_SIZE, ROWS), F32),
            jax.ShapeDtypeStruct(kv.shape, BF16),
        ),
        in_specs=[SCALARS] + [WHOLE] * len(args),
        out_specs=(WHOLE, WHOLE),
        scratch_shapes=[
            pltpu.VMEM((ROWS, HEAD_SIZE), BF16),
            pltpu.VMEM((ROWS, HEAD_SIZE), BF16),
        ],
        compiler_params=pltpu.CompilerParams(vmem_limit_bytes=18 * 2**20),
        cost_estimate=pl.CostEstimate(
            flops=12 * ROWS * SLABS * keys * HEAD_SIZE, bytes_accessed=4 * 2**20, transcendentals=ROWS
        ),
        name="attention_gradients",
    )(place, *args)


def line_lists(ctx_count, tp_count, along_z):
    span = ctx_count // GROUPS
    plane = span // SLABS
    lists = []
    for t in range(tp_count):
        first = span // 2 if t >= tp_count // 2 and along_z else 0
        for g in range(GROUPS):
            if along_z:
                lines = [[first + g * span + s * plane + p for s in range(SLABS)] for p in range(plane)]
            else:
                lines = [
                    [g * span + s * plane + y * PAIR + x for y in range(plane // PAIR)]
                    for s in range(SLABS)
                    for x in range(PAIR)
                ]
            lists += [[c % ctx_count * tp_count + t for c in line] for line in lines]
    return lists


def exchange(parts, lists):
    return lax.all_to_all(parts, AXES, 0, 0, axis_index_groups=lists, tiled=True)


def to_peer(array):
    return lax.ppermute(array, "ctx", [(c, c ^ 1) for c in range(lax.axis_size("ctx"))])


def shards(query_heads, key_heads_wide, value_heads_wide, grad_output):
    ctx_count = lax.axis_size("ctx")
    tp_count = lax.axis_size("tp")
    span = ctx_count // GROUPS
    plane = span // SLABS
    lines = plane // PAIR
    here = key_heads_wide.shape[0]
    rows = query_heads.shape[0]
    along_z = line_lists(ctx_count, tp_count, True)
    along_y = line_lists(ctx_count, tp_count, False)
    offset = jnp.where(lax.axis_index("tp") >= tp_count // 2, span // 2, 0)
    rank = (jnp.mod(lax.axis_index("ctx") - offset, ctx_count) % span).astype(jnp.int32)
    place = jnp.stack([rank // plane, rank % plane // PAIR, rank % PAIR])

    peer_q, peer_do = to_peer(query_heads), to_peer(grad_output)
    shape = jax.ShapeDtypeStruct((ROWS, HEAD_SIZE), BF16)
    own_q, own_do = small(
        rows_kernel, "queries_by_head", (shape, shape), [WHOLE] * 2, (WHOLE, WHOLE), [], 4, query_heads, grad_output
    )
    is_value = lax.broadcasted_iota(jnp.int32, (2,) + key_heads_wide.shape, 0) == 1
    both = small(
        pack_kernel, "keys_and_values_by_head", jax.ShapeDtypeStruct((tp_count, here, 2 * HEAD_SIZE), BF16),
        [WHOLE], WHOLE, [], 4, jnp.where(is_value, value_heads_wide, key_heads_wide),
    )
    own = lax.all_to_all(both, "tp", 0, 0, tiled=True).reshape(rows, 2 * HEAD_SIZE)
    column = exchange(jnp.broadcast_to(own, (SLABS,) + own.shape), along_z)
    kv = exchange(jnp.broadcast_to(column, (lines,) + column.shape), along_y)
    own_stats, *own_held = row_statistics(False, place, own_q, own_do, kv)
    stats, *peer_held = row_statistics(True, place, peer_q, peer_do, kv, own_stats)
    k_cols = small(
        key_columns_kernel, "keys_by_column",
        jax.ShapeDtypeStruct((SLABS, HEAD_SIZE, kv.shape[0] * rows), BF16), [WHOLE], WHOLE, [], 4, kv,
    )
    dq_cols, dkv = attention_gradients(
        place, own_q, own_do, peer_q, peer_do, kv, stats, to_peer(stats), *own_held, *peer_held, k_cols
    )
    shape = query_heads.shape
    dq, dq_peer = small(
        query_rows_kernel, "query_gradients_by_token",
        (jax.ShapeDtypeStruct(shape, F32), jax.ShapeDtypeStruct(shape, BF16)), [WHOLE], (WHOLE, WHOLE), [], 8, dq_cols,
    )
    dq_there = to_peer(dq_peer)
    partial = summed(exchange(dkv, along_y), BF16)
    mine = summed(exchange(partial, along_z), F32)
    back = lax.all_to_all(mine.reshape(tp_count, here, 2 * HEAD_SIZE), "tp", 0, 0, tiled=True)
    shape = jax.ShapeDtypeStruct(key_heads_wide.shape, F32)
    key_gradient, value_gradient, grad_query = small(
        finish_kernel, "gradients_by_token", (shape, shape, jax.ShapeDtypeStruct(dq.shape, F32)),
        [WHOLE] * 3, (IN_HBM,) * 3,
        [pltpu.VMEM(dq.shape, F32), pltpu.SemaphoreType.DMA((3, tp_count))], 4, back, dq, dq_there,
    )
    return grad_query, key_gradient, value_gradient


def solution(mesh):
    return jax.shard_map(
        shards,
        mesh=mesh,
        in_specs=(P("ctx", "tp"), P(AXES, None), P(AXES, None), P("ctx", "tp")),
        out_specs=(P("ctx", "tp"), P(AXES, None), P(AXES, None)),
        check_vma=False,
    )
```

```python
import functools
import math

import jax
import jax.numpy as jnp
from jax import lax
from jax.experimental import pallas as pl
from jax.experimental.pallas import tpu as pltpu
from jax.sharding import PartitionSpec as P

HEAD_SIZE = 128
GROUPS = 4
SLABS = 4
PAIR = 2
ROWS = 1024
LOWEST = -1e30
AXES = ("ctx", "tp")
BF16, F32 = jnp.bfloat16, jnp.float32
SCALE = 1.0 / math.sqrt(HEAD_SIZE)


def product(a, b):
    return jnp.dot(a, b, preferred_element_type=F32)


def product_of_rows(a, b):
    return lax.dot_general(a, b, (((1,), (1,)), ((), ())), preferred_element_type=F32)


def keys_of(kv_ref, slab, column):
    part = kv_ref[:, slab, :, column * HEAD_SIZE : (column + 1) * HEAD_SIZE]
    return part.reshape(part.shape[0] * part.shape[1], HEAD_SIZE)


def by_head(ref, out):
    tokens = ref.shape[0]
    for h in range(ref.shape[1] // HEAD_SIZE):
        out[h * tokens : (h + 1) * tokens, :] = ref[:, h * HEAD_SIZE : (h + 1) * HEAD_SIZE]


def row_of(ref, i, tile):
    width = ref.shape[1]
    first = 8 * i + tile * (ROWS // width)
    return jnp.concatenate([ref[r : r + 1, :] for r in range(first, first + ROWS // width)], axis=1)


def rows_kernel(q_ref, do_ref, q_rows, do_rows):
    by_head(q_ref, q_rows)
    by_head(do_ref, do_rows)


def statistics_kernel(of_peer, place_ref, *refs):
    if of_peer:
        q_ref, do_ref, kv_ref, own_stats, stats_ref, maxima_ref, weights_ref, slopes_ref, q_rows, do_rows = refs
        rows_kernel(q_ref, do_ref, q_rows, do_rows)
        stats_ref[...] = own_stats[...]
    else:
        q_rows, do_rows, kv_ref, stats_ref, maxima_ref, weights_ref, slopes_ref = refs
    tokens = kv_ref.shape[2]
    keys = kv_ref.shape[0] * kv_ref.shape[2]
    slab, along_y, along_x = place_ref[0], place_ref[1], place_ref[2]

    def step(s, carry, masked):
        highest, norm, weighted = carry
        scores = product_of_rows(keys_of(kv_ref, s, 0), q_rows[...]) * (SCALE * math.log2(math.e))
        if masked:
            key = lax.broadcasted_iota(jnp.int32, (keys, ROWS), 0)
            if of_peer:
                last = (along_y + 1 - along_x) * tokens - 1
            else:
                token = lax.rem(lax.broadcasted_iota(jnp.int32, (keys, ROWS), 1), jnp.int32(tokens))
                last = along_y * tokens + token
            scores = jnp.where(key <= last, scores, LOWEST)
        higher = jnp.maximum(highest, jnp.max(scores, axis=0, keepdims=True))
        weight = jnp.exp2(scores - higher)
        factor = jnp.exp2(highest - higher)
        slope = product_of_rows(keys_of(kv_ref, s, 1), do_rows[...])
        weights_ref[s] = weight.astype(BF16)
        slopes_ref[s] = slope
        maxima_ref[pl.ds(s, 1), :] = higher
        norm = norm * factor + jnp.sum(weight, axis=0, keepdims=True)
        weighted = weighted * factor + jnp.sum(weight * slope, axis=0, keepdims=True)
        return higher, norm, weighted

    def finish(carry):
        width = stats_ref.shape[1]
        for i, row in enumerate(step(slab, carry, True)):
            for j in range(ROWS // width):
                at = 8 * i + of_peer * (ROWS // width) + j
                stats_ref[at : at + 1, :] = row[:, j * width : (j + 1) * width]

    zeros = jnp.zeros((1, ROWS), F32)
    start = (jnp.full((1, ROWS), LOWEST, F32), zeros, zeros)

    @pl.when(slab == SLABS - 1)
    def _():
        carry = start
        for s in range(SLABS - 1):
            carry = step(s, carry, False)
        finish(carry)

    @pl.when(slab < SLABS - 1)
    def _():
        finish(lax.fori_loop(0, slab, functools.partial(step, masked=False), start))


def key_columns_kernel(kv_ref, k_cols):
    for s in range(SLABS):
        k_cols[s] = keys_of(kv_ref, s, 0).T


def query_rows_kernel(cols_ref, dq_ref, dq_peer_ref):
    tokens = dq_ref.shape[0]
    for owner, out in enumerate((dq_ref, dq_peer_ref)):
        for h in range(dq_ref.shape[1] // HEAD_SIZE):
            part = cols_ref[owner, :, h * tokens : (h + 1) * tokens].T
            out[:, h * HEAD_SIZE : (h + 1) * HEAD_SIZE] = part.astype(out.dtype)


def gradients_kernel(
    place_ref, own_q, own_do, peer_q, peer_do, kv_ref, stats_ref, other_ref,
    own_maxima, own_weights, own_slopes, peer_maxima, peer_weights, peer_slopes,
    k_cols, dq_ref, dkv_out,
    there_q, there_do, dkv_ref, sems,
):
    tokens = peer_q.shape[0]
    along_y = kv_ref.shape[0]
    slab = place_ref[0]
    rows_kernel(peer_q, peer_do, there_q, there_do)

    rows = ((own_q, own_do), (there_q, there_do))
    held = ((own_maxima, own_weights, own_slopes), (peer_maxima, peer_weights, peer_slopes))
    norms = []
    for owner in range(PAIR):
        here_highest, there_highest = row_of(stats_ref, 0, owner), row_of(other_ref, 0, 1 - owner)
        highest = jnp.maximum(here_highest, there_highest)
        here_factor, there_factor = jnp.exp2(here_highest - highest), jnp.exp2(there_highest - highest)
        inverse = 1.0 / (row_of(stats_ref, 1, owner) * here_factor + row_of(other_ref, 1, 1 - owner) * there_factor)
        centre = row_of(stats_ref, 2, owner) * here_factor + row_of(other_ref, 2, 1 - owner) * there_factor
        norms.append((highest, inverse, centre * inverse))

    def leaving(s):
        return pltpu.make_async_copy(dkv_ref.at[:, s], dkv_out.at[:, s], sems.at[s])

    def step(s, dq_cols):
        dk = dv = 0.0
        added = []
        for owner in range(PAIR):
            (q_rows, do_rows), (maxima, weights, slopes) = rows[owner], held[owner]
            highest, inverse, centre = norms[owner]
            factor = jnp.exp2(maxima[pl.ds(s, 1), :] - highest) * inverse
            soft = weights[s].astype(F32) * factor
            score_grad = (soft * (slopes[s] - centre)).astype(BF16)
            dk += product(score_grad, q_rows[...])
            dv += product(soft.astype(BF16), do_rows[...])
            added.append(dq_cols[owner] + product(k_cols[s], score_grad))
        dkv_ref[:, s, :, 0:HEAD_SIZE] = (dk * SCALE).astype(BF16).reshape(along_y, tokens, HEAD_SIZE)
        dkv_ref[:, s, :, HEAD_SIZE:] = dv.astype(BF16).reshape(along_y, tokens, HEAD_SIZE)
        leaving(s).start()
        return tuple(added)

    def finish(dq_cols):
        for owner in range(PAIR):
            dq_ref[owner] = dq_cols[owner] * SCALE

    start = (jnp.zeros((HEAD_SIZE, ROWS), F32),) * PAIR

    @pl.when(slab == SLABS - 1)
    def _():
        dq_cols = start
        for s in range(SLABS):
            dq_cols = step(s, dq_cols)
        finish(dq_cols)

    @pl.when(slab < SLABS - 1)
    def _():
        finish(lax.fori_loop(0, slab + 1, step, start))

        @pl.loop(slab + 1, SLABS)
        def _(s):
            dkv_ref[:, s] = jnp.zeros((along_y, tokens, 2 * HEAD_SIZE), BF16)
            leaving(s).start()

    for s in range(SLABS):
        leaving(s).wait()


def pack_kernel(both_ref, out_ref):
    for h in range(out_ref.shape[0]):
        for i in range(2):
            out_ref[h, :, i * HEAD_SIZE : (i + 1) * HEAD_SIZE] = both_ref[i, :, h * HEAD_SIZE : (h + 1) * HEAD_SIZE]


def finish_kernel(both_ref, dq_ref, peer_ref, key_ref, value_ref, query_ref, total, sems):
    heads = both_ref.shape[0]
    copies = [
        pltpu.make_async_copy(
            both_ref.at[h, :, i * HEAD_SIZE : (i + 1) * HEAD_SIZE],
            ref.at[:, h * HEAD_SIZE : (h + 1) * HEAD_SIZE],
            sems.at[i, h],
        )
        for i, ref in enumerate((key_ref, value_ref))
        for h in range(heads)
    ]
    for copy in copies:
        copy.start()
    tokens = total.shape[0] // heads
    for h in range(heads):
        down = slice(h * tokens, (h + 1) * tokens)
        total[down, :] = dq_ref[down, :] + peer_ref[down, :].astype(F32)
        copies.append(pltpu.make_async_copy(total.at[down, :], query_ref.at[down, :], sems.at[2, h]))
        copies[-1].start()
    for copy in copies:
        copy.wait()


def sum_kernel(parts_ref, out_ref):
    total = parts_ref[0].astype(F32)
    for i in range(1, parts_ref.shape[0]):
        total += parts_ref[i].astype(F32)
    out_ref[...] = total.astype(out_ref.dtype)


WHOLE = pl.BlockSpec(memory_space=pltpu.VMEM)
IN_HBM = pl.BlockSpec(memory_space=pltpu.HBM)


def small(kernel, name, out, in_specs, out_specs, scratch, room, *args):
    moved = sum(a.size * a.dtype.itemsize for a in args)
    return pl.pallas_call(
        kernel,
        out_shape=out,
        in_specs=in_specs,
        out_specs=out_specs,
        scratch_shapes=scratch,
        compiler_params=pltpu.CompilerParams(vmem_limit_bytes=room * 2**20),
        cost_estimate=pl.CostEstimate(flops=0, bytes_accessed=2 * moved, transcendentals=0),
        name=name,
    )(*args)


def summed(parts, dtype):
    shape = jax.ShapeDtypeStruct(parts.shape[1:], dtype)
    return small(sum_kernel, "sum_of_parts", shape, [WHOLE], WHOLE, [], 4, parts)
SCALARS = pl.BlockSpec(memory_space=pltpu.SMEM)


def row_statistics(of_peer, place, q, do, kv, *own_stats):
    keys = kv.shape[0] * kv.shape[2]
    return pl.pallas_call(
        functools.partial(statistics_kernel, of_peer),
        out_shape=(
            jax.ShapeDtypeStruct((24, PAIR * ROWS // 8), F32),
            jax.ShapeDtypeStruct((8, ROWS), F32),
            jax.ShapeDtypeStruct((SLABS, keys, ROWS), BF16),
            jax.ShapeDtypeStruct((SLABS, keys, ROWS), F32),
        ),
        in_specs=[SCALARS] + [WHOLE] * (3 + len(own_stats)),
        out_specs=(WHOLE,) * 4,
        scratch_shapes=[pltpu.VMEM((ROWS, HEAD_SIZE), BF16)] * 2 if of_peer else [],
        compiler_params=pltpu.CompilerParams(vmem_limit_bytes=12 * 2**20),
        cost_estimate=pl.CostEstimate(
            flops=4 * ROWS * SLABS * keys * HEAD_SIZE, bytes_accessed=2**20, transcendentals=ROWS * SLABS * keys
        ),
        name="row_statistics",
    )(place, q, do, kv, *own_stats)


def attention_gradients(place, *args):
    kv = args[4]
    keys = kv.shape[0] * kv.shape[2]
    return pl.pallas_call(
        gradients_kernel,
        out_shape=(
            jax.ShapeDtypeStruct((PAIR, HEAD_SIZE, ROWS), F32),
            jax.ShapeDtypeStruct(kv.shape, BF16),
        ),
        in_specs=[SCALARS] + [WHOLE] * len(args),
        out_specs=(WHOLE, IN_HBM),
        scratch_shapes=[
            pltpu.VMEM((ROWS, HEAD_SIZE), BF16),
            pltpu.VMEM((ROWS, HEAD_SIZE), BF16),
            pltpu.VMEM(kv.shape, BF16),
            pltpu.SemaphoreType.DMA((SLABS,)),
        ],
        compiler_params=pltpu.CompilerParams(vmem_limit_bytes=19 * 2**20),
        cost_estimate=pl.CostEstimate(
            flops=12 * ROWS * SLABS * keys * HEAD_SIZE, bytes_accessed=4 * 2**20, transcendentals=ROWS
        ),
        name="attention_gradients",
    )(place, *args)


def line_lists(ctx_count, tp_count, along_z):
    span = ctx_count // GROUPS
    plane = span // SLABS
    lists = []
    for t in range(tp_count):
        first = span // 2 if t >= tp_count // 2 and along_z else 0
        for g in range(GROUPS):
            if along_z:
                lines = [[first + g * span + s * plane + p for s in range(SLABS)] for p in range(plane)]
            else:
                lines = [
                    [g * span + s * plane + y * PAIR + x for y in range(plane // PAIR)]
                    for s in range(SLABS)
                    for x in range(PAIR)
                ]
            lists += [[c % ctx_count * tp_count + t for c in line] for line in lines]
    return lists


def exchange(parts, lists):
    return lax.all_to_all(parts, AXES, 0, 0, axis_index_groups=lists, tiled=True)


def to_peer(array):
    return lax.ppermute(array, "ctx", [(c, c ^ 1) for c in range(lax.axis_size("ctx"))])


def shards(query_heads, key_heads_wide, value_heads_wide, grad_output):
    ctx_count = lax.axis_size("ctx")
    tp_count = lax.axis_size("tp")
    span = ctx_count // GROUPS
    plane = span // SLABS
    lines = plane // PAIR
    here = key_heads_wide.shape[0]
    rows = query_heads.shape[0]
    along_z = line_lists(ctx_count, tp_count, True)
    along_y = line_lists(ctx_count, tp_count, False)
    offset = jnp.where(lax.axis_index("tp") >= tp_count // 2, span // 2, 0)
    rank = (jnp.mod(lax.axis_index("ctx") - offset, ctx_count) % span).astype(jnp.int32)
    place = jnp.stack([rank // plane, rank % plane // PAIR, rank % PAIR])

    peer_q, peer_do = to_peer(query_heads), to_peer(grad_output)
    shape = jax.ShapeDtypeStruct((ROWS, HEAD_SIZE), BF16)
    own_q, own_do = small(
        rows_kernel, "queries_by_head", (shape, shape), [WHOLE] * 2, (WHOLE, WHOLE), [], 4, query_heads, grad_output
    )
    is_value = lax.broadcasted_iota(jnp.int32, (2,) + key_heads_wide.shape, 0) == 1
    both = small(
        pack_kernel, "keys_and_values_by_head", jax.ShapeDtypeStruct((tp_count, here, 2 * HEAD_SIZE), BF16),
        [WHOLE], WHOLE, [], 4, jnp.where(is_value, value_heads_wide, key_heads_wide),
    )
    own = lax.all_to_all(both, "tp", 0, 0, tiled=True).reshape(rows, 2 * HEAD_SIZE)
    column = exchange(jnp.broadcast_to(own, (SLABS,) + own.shape), along_z)
    kv = exchange(jnp.broadcast_to(column, (lines,) + column.shape), along_y)
    own_stats, *own_held = row_statistics(False, place, own_q, own_do, kv)
    stats, *peer_held = row_statistics(True, place, peer_q, peer_do, kv, own_stats)
    k_cols = small(
        key_columns_kernel, "keys_by_column",
        jax.ShapeDtypeStruct((SLABS, HEAD_SIZE, kv.shape[0] * rows), BF16), [WHOLE], WHOLE, [], 4, kv,
    )
    dq_cols, dkv = attention_gradients(
        place, own_q, own_do, peer_q, peer_do, kv, stats, to_peer(stats), *own_held, *peer_held, k_cols
    )
    shape = query_heads.shape
    dq, dq_peer = small(
        query_rows_kernel, "query_gradients_by_token",
        (jax.ShapeDtypeStruct(shape, F32), jax.ShapeDtypeStruct(shape, BF16)), [WHOLE], (WHOLE, WHOLE), [], 8, dq_cols,
    )
    dq_there = to_peer(dq_peer)
    partial = summed(exchange(dkv, along_y), BF16)
    partial, dq_there = lax.optimization_barrier((partial, dq_there))
    mine = summed(exchange(partial, along_z), F32)
    back = lax.all_to_all(mine.reshape(tp_count, here, 2 * HEAD_SIZE), "tp", 0, 0, tiled=True)
    shape = jax.ShapeDtypeStruct(key_heads_wide.shape, F32)
    key_gradient, value_gradient, grad_query = small(
        finish_kernel, "gradients_by_token", (shape, shape, jax.ShapeDtypeStruct(dq.shape, F32)),
        [WHOLE] * 3, (IN_HBM,) * 3,
        [pltpu.VMEM(dq.shape, F32), pltpu.SemaphoreType.DMA((3, tp_count))], 4, back, dq, dq_there,
    )
    return grad_query, key_gradient, value_gradient


def solution(mesh):
    return jax.shard_map(
        shards,
        mesh=mesh,
        in_specs=(P("ctx", "tp"), P(AXES, None), P(AXES, None), P("ctx", "tp")),
        out_specs=(P("ctx", "tp"), P(AXES, None), P(AXES, None)),
        check_vma=False,
    )
```

```python
import functools
import math

import jax
import jax.numpy as jnp
from jax import lax
from jax.experimental import pallas as pl
from jax.experimental.pallas import tpu as pltpu
from jax.sharding import PartitionSpec as P

HEAD_SIZE = 128
GROUPS = 4
SLABS = 4
PAIR = 2
ROWS = 1024
LOWEST = -1e30
AXES = ("ctx", "tp")
BF16, F32 = jnp.bfloat16, jnp.float32
SCALE = 1.0 / math.sqrt(HEAD_SIZE)


def product(a, b):
    return jnp.dot(a, b, preferred_element_type=F32)


def product_of_rows(a, b):
    return lax.dot_general(a, b, (((1,), (1,)), ((), ())), preferred_element_type=F32)


def keys_of(kv_ref, slab, column):
    part = kv_ref[:, slab, :, column * HEAD_SIZE : (column + 1) * HEAD_SIZE]
    return part.reshape(part.shape[0] * part.shape[1], HEAD_SIZE)


def by_head(ref, out):
    tokens = ref.shape[0]
    for h in range(ref.shape[1] // HEAD_SIZE):
        out[h * tokens : (h + 1) * tokens, :] = ref[:, h * HEAD_SIZE : (h + 1) * HEAD_SIZE]


def row_of(ref, i, tile):
    width = ref.shape[1]
    first = 8 * i + tile * (ROWS // width)
    return jnp.concatenate([ref[r : r + 1, :] for r in range(first, first + ROWS // width)], axis=1)


def rows_kernel(q_ref, do_ref, q_rows, do_rows):
    by_head(q_ref, q_rows)
    by_head(do_ref, do_rows)


def statistics_kernel(of_peer, place_ref, *refs):
    if of_peer:
        q_ref, do_ref, kv_ref, own_stats, stats_ref, maxima_ref, weights_ref, slopes_ref, q_rows, do_rows = refs
        rows_kernel(q_ref, do_ref, q_rows, do_rows)
        stats_ref[...] = own_stats[...]
    else:
        q_rows, do_rows, kv_ref, stats_ref, maxima_ref, weights_ref, slopes_ref = refs
    tokens = kv_ref.shape[2]
    keys = kv_ref.shape[0] * kv_ref.shape[2]
    slab, along_y, along_x = place_ref[0], place_ref[1], place_ref[2]

    def step(s, carry, masked):
        highest, norm, weighted = carry
        scores = product_of_rows(keys_of(kv_ref, s, 0), q_rows[...]) * (SCALE * math.log2(math.e))
        if masked:
            key = lax.broadcasted_iota(jnp.int32, (keys, ROWS), 0)
            if of_peer:
                last = (along_y + 1 - along_x) * tokens - 1
            else:
                token = lax.rem(lax.broadcasted_iota(jnp.int32, (keys, ROWS), 1), jnp.int32(tokens))
                last = along_y * tokens + token
            scores = jnp.where(key <= last, scores, LOWEST)
        higher = jnp.maximum(highest, jnp.max(scores, axis=0, keepdims=True))
        weight = jnp.exp2(scores - higher)
        factor = jnp.exp2(highest - higher)
        slope = product_of_rows(keys_of(kv_ref, s, 1), do_rows[...])
        weights_ref[s] = weight.astype(BF16)
        slopes_ref[s] = slope
        maxima_ref[pl.ds(s, 1), :] = higher
        norm = norm * factor + jnp.sum(weight, axis=0, keepdims=True)
        weighted = weighted * factor + jnp.sum(weight * slope, axis=0, keepdims=True)
        return higher, norm, weighted

    def finish(carry):
        width = stats_ref.shape[1]
        for i, row in enumerate(step(slab, carry, True)):
            for j in range(ROWS // width):
                at = 8 * i + of_peer * (ROWS // width) + j
                stats_ref[at : at + 1, :] = row[:, j * width : (j + 1) * width]

    zeros = jnp.zeros((1, ROWS), F32)
    start = (jnp.full((1, ROWS), LOWEST, F32), zeros, zeros)

    @pl.when(slab == SLABS - 1)
    def _():
        carry = start
        for s in range(SLABS - 1):
            carry = step(s, carry, False)
        finish(carry)

    @pl.when(slab < SLABS - 1)
    def _():
        finish(lax.fori_loop(0, slab, functools.partial(step, masked=False), start))


def key_columns_kernel(kv_ref, k_cols):
    for s in range(SLABS):
        k_cols[s] = keys_of(kv_ref, s, 0).T


def query_rows_kernel(cols_ref, dq_ref, dq_peer_ref):
    tokens = dq_ref.shape[0]
    for owner, out in enumerate((dq_ref, dq_peer_ref)):
        for h in range(dq_ref.shape[1] // HEAD_SIZE):
            part = cols_ref[owner, :, h * tokens : (h + 1) * tokens].T
            out[:, h * HEAD_SIZE : (h + 1) * HEAD_SIZE] = part.astype(out.dtype)


def gradients_kernel(
    place_ref, own_q, own_do, peer_q, peer_do, kv_ref, stats_ref, other_ref,
    own_maxima, own_weights, own_slopes, peer_maxima, peer_weights, peer_slopes,
    k_cols, dq_ref, dkv_ref,
    there_q, there_do,
):
    tokens = peer_q.shape[0]
    along_y = kv_ref.shape[0]
    slab = place_ref[0]
    rows_kernel(peer_q, peer_do, there_q, there_do)

    rows = ((own_q, own_do), (there_q, there_do))
    held = ((own_maxima, own_weights, own_slopes), (peer_maxima, peer_weights, peer_slopes))
    norms = []
    for owner in range(PAIR):
        here_highest, there_highest = row_of(stats_ref, 0, owner), row_of(other_ref, 0, 1 - owner)
        highest = jnp.maximum(here_highest, there_highest)
        here_factor, there_factor = jnp.exp2(here_highest - highest), jnp.exp2(there_highest - highest)
        inverse = 1.0 / (row_of(stats_ref, 1, owner) * here_factor + row_of(other_ref, 1, 1 - owner) * there_factor)
        centre = row_of(stats_ref, 2, owner) * here_factor + row_of(other_ref, 2, 1 - owner) * there_factor
        norms.append((highest, inverse, centre * inverse))

    def step(s, dq_cols):
        dk = dv = 0.0
        added = []
        for owner in range(PAIR):
            (q_rows, do_rows), (maxima, weights, slopes) = rows[owner], held[owner]
            highest, inverse, centre = norms[owner]
            factor = jnp.exp2(maxima[pl.ds(s, 1), :] - highest) * inverse
            soft = weights[s].astype(F32) * factor
            score_grad = (soft * (slopes[s] - centre)).astype(BF16)
            dk += product(score_grad, q_rows[...])
            dv += product(soft.astype(BF16), do_rows[...])
            added.append(dq_cols[owner] + product(k_cols[s], score_grad))
        dkv_ref[:, s, :, 0:HEAD_SIZE] = (dk * SCALE).astype(BF16).reshape(along_y, tokens, HEAD_SIZE)
        dkv_ref[:, s, :, HEAD_SIZE:] = dv.astype(BF16).reshape(along_y, tokens, HEAD_SIZE)
        return tuple(added)

    def finish(dq_cols):
        for owner in range(PAIR):
            dq_ref[owner] = dq_cols[owner] * SCALE

    start = (jnp.zeros((HEAD_SIZE, ROWS), F32),) * PAIR

    @pl.when(slab == SLABS - 1)
    def _():
        dq_cols = start
        for s in range(SLABS):
            dq_cols = step(s, dq_cols)
        finish(dq_cols)

    @pl.when(slab < SLABS - 1)
    def _():
        finish(lax.fori_loop(0, slab + 1, step, start))

        @pl.loop(slab + 1, SLABS)
        def _(s):
            dkv_ref[:, s] = jnp.zeros((along_y, tokens, 2 * HEAD_SIZE), BF16)


def pack_kernel(both_ref, out_ref):
    for h in range(out_ref.shape[0]):
        for i in range(2):
            out_ref[h, :, i * HEAD_SIZE : (i + 1) * HEAD_SIZE] = both_ref[i, :, h * HEAD_SIZE : (h + 1) * HEAD_SIZE]


def finish_kernel(both_ref, dq_ref, peer_ref, key_ref, value_ref, query_ref, wide, total, sems):
    heads = both_ref.shape[0]
    copies = []
    for i, ref in enumerate((key_ref, value_ref)):
        for h in range(heads):
            part = both_ref[h, :, i * HEAD_SIZE : (i + 1) * HEAD_SIZE]
            wide[i, :, h * HEAD_SIZE : (h + 1) * HEAD_SIZE] = part.astype(F32)
        copies.append(pltpu.make_async_copy(wide.at[i], ref, sems.at[i, 0]))
        copies[-1].start()
    tokens = total.shape[0] // heads
    for h in range(heads):
        down = slice(h * tokens, (h + 1) * tokens)
        total[down, :] = dq_ref[down, :] + peer_ref[down, :].astype(F32)
        copies.append(pltpu.make_async_copy(total.at[down, :], query_ref.at[down, :], sems.at[2, h]))
        copies[-1].start()
    for copy in copies:
        copy.wait()


def sum_kernel(parts_ref, out_ref):
    total = parts_ref[0].astype(F32)
    for i in range(1, parts_ref.shape[0]):
        total += parts_ref[i].astype(F32)
    out_ref[...] = total.astype(out_ref.dtype)


WHOLE = pl.BlockSpec(memory_space=pltpu.VMEM)
IN_HBM = pl.BlockSpec(memory_space=pltpu.HBM)


def small(kernel, name, out, in_specs, out_specs, scratch, room, *args):
    moved = sum(a.size * a.dtype.itemsize for a in args)
    return pl.pallas_call(
        kernel,
        out_shape=out,
        in_specs=in_specs,
        out_specs=out_specs,
        scratch_shapes=scratch,
        compiler_params=pltpu.CompilerParams(vmem_limit_bytes=room * 2**20),
        cost_estimate=pl.CostEstimate(flops=0, bytes_accessed=2 * moved, transcendentals=0),
        name=name,
    )(*args)


def summed(parts, dtype):
    shape = jax.ShapeDtypeStruct(parts.shape[1:], dtype)
    return small(sum_kernel, "sum_of_parts", shape, [WHOLE], WHOLE, [], 4, parts)
SCALARS = pl.BlockSpec(memory_space=pltpu.SMEM)


def row_statistics(of_peer, place, q, do, kv, *own_stats):
    keys = kv.shape[0] * kv.shape[2]
    return pl.pallas_call(
        functools.partial(statistics_kernel, of_peer),
        out_shape=(
            jax.ShapeDtypeStruct((24, PAIR * ROWS // 8), F32),
            jax.ShapeDtypeStruct((8, ROWS), F32),
            jax.ShapeDtypeStruct((SLABS, keys, ROWS), BF16),
            jax.ShapeDtypeStruct((SLABS, keys, ROWS), F32),
        ),
        in_specs=[SCALARS] + [WHOLE] * (3 + len(own_stats)),
        out_specs=(WHOLE,) * 4,
        scratch_shapes=[pltpu.VMEM((ROWS, HEAD_SIZE), BF16)] * 2 if of_peer else [],
        compiler_params=pltpu.CompilerParams(vmem_limit_bytes=12 * 2**20),
        cost_estimate=pl.CostEstimate(
            flops=4 * ROWS * SLABS * keys * HEAD_SIZE, bytes_accessed=2**20, transcendentals=ROWS * SLABS * keys
        ),
        name="row_statistics",
    )(place, q, do, kv, *own_stats)


def attention_gradients(place, *args):
    kv = args[4]
    keys = kv.shape[0] * kv.shape[2]
    return pl.pallas_call(
        gradients_kernel,
        out_shape=(
            jax.ShapeDtypeStruct((PAIR, HEAD_SIZE, ROWS), F32),
            jax.ShapeDtypeStruct(kv.shape, BF16),
        ),
        in_specs=[SCALARS] + [WHOLE] * len(args),
        out_specs=(WHOLE, WHOLE),
        scratch_shapes=[
            pltpu.VMEM((ROWS, HEAD_SIZE), BF16),
            pltpu.VMEM((ROWS, HEAD_SIZE), BF16),
        ],
        compiler_params=pltpu.CompilerParams(vmem_limit_bytes=18 * 2**20),
        cost_estimate=pl.CostEstimate(
            flops=12 * ROWS * SLABS * keys * HEAD_SIZE, bytes_accessed=4 * 2**20, transcendentals=ROWS
        ),
        name="attention_gradients",
    )(place, *args)


def line_lists(ctx_count, tp_count, along_z):
    span = ctx_count // GROUPS
    plane = span // SLABS
    lists = []
    for t in range(tp_count):
        first = span // 2 if t >= tp_count // 2 and along_z else 0
        for g in range(GROUPS):
            if along_z:
                lines = [[first + g * span + s * plane + p for s in range(SLABS)] for p in range(plane)]
            else:
                lines = [
                    [g * span + s * plane + y * PAIR + x for y in range(plane // PAIR)]
                    for s in range(SLABS)
                    for x in range(PAIR)
                ]
            lists += [[c % ctx_count * tp_count + t for c in line] for line in lines]
    return lists


def exchange(parts, lists):
    return lax.all_to_all(parts, AXES, 0, 0, axis_index_groups=lists, tiled=True)


def to_peer(array):
    return lax.ppermute(array, "ctx", [(c, c ^ 1) for c in range(lax.axis_size("ctx"))])


def shards(query_heads, key_heads_wide, value_heads_wide, grad_output):
    ctx_count = lax.axis_size("ctx")
    tp_count = lax.axis_size("tp")
    span = ctx_count // GROUPS
    plane = span // SLABS
    lines = plane // PAIR
    here = key_heads_wide.shape[0]
    rows = query_heads.shape[0]
    along_z = line_lists(ctx_count, tp_count, True)
    along_y = line_lists(ctx_count, tp_count, False)
    offset = jnp.where(lax.axis_index("tp") >= tp_count // 2, span // 2, 0)
    rank = (jnp.mod(lax.axis_index("ctx") - offset, ctx_count) % span).astype(jnp.int32)
    place = jnp.stack([rank // plane, rank % plane // PAIR, rank % PAIR])

    peer_q, peer_do = to_peer(query_heads), to_peer(grad_output)
    shape = jax.ShapeDtypeStruct((ROWS, HEAD_SIZE), BF16)
    own_q, own_do = small(
        rows_kernel, "queries_by_head", (shape, shape), [WHOLE] * 2, (WHOLE, WHOLE), [], 4, query_heads, grad_output
    )
    is_value = lax.broadcasted_iota(jnp.int32, (2,) + key_heads_wide.shape, 0) == 1
    both = small(
        pack_kernel, "keys_and_values_by_head", jax.ShapeDtypeStruct((tp_count, here, 2 * HEAD_SIZE), BF16),
        [WHOLE], WHOLE, [], 4, jnp.where(is_value, value_heads_wide, key_heads_wide),
    )
    own = lax.all_to_all(both, "tp", 0, 0, tiled=True).reshape(rows, 2 * HEAD_SIZE)
    column = exchange(jnp.broadcast_to(own, (SLABS,) + own.shape), along_z)
    kv = exchange(jnp.broadcast_to(column, (lines,) + column.shape), along_y)
    own_stats, *own_held = row_statistics(False, place, own_q, own_do, kv)
    stats, *peer_held = row_statistics(True, place, peer_q, peer_do, kv, own_stats)
    k_cols = small(
        key_columns_kernel, "keys_by_column",
        jax.ShapeDtypeStruct((SLABS, HEAD_SIZE, kv.shape[0] * rows), BF16), [WHOLE], WHOLE, [], 4, kv,
    )
    dq_cols, dkv = attention_gradients(
        place, own_q, own_do, peer_q, peer_do, kv, stats, to_peer(stats), *own_held, *peer_held, k_cols
    )
    shape = query_heads.shape
    dq, dq_peer = small(
        query_rows_kernel, "query_gradients_by_token",
        (jax.ShapeDtypeStruct(shape, F32), jax.ShapeDtypeStruct(shape, BF16)), [WHOLE], (WHOLE, WHOLE), [], 8, dq_cols,
    )
    dq_there = to_peer(dq_peer)
    partial = summed(exchange(dkv, along_y), BF16)
    mine = summed(exchange(partial, along_z), BF16)
    back = lax.all_to_all(mine.reshape(tp_count, here, 2 * HEAD_SIZE), "tp", 0, 0, tiled=True)
    shape = jax.ShapeDtypeStruct(key_heads_wide.shape, F32)
    key_gradient, value_gradient, grad_query = small(
        finish_kernel, "gradients_by_token", (shape, shape, jax.ShapeDtypeStruct(dq.shape, F32)),
        [WHOLE] * 3, (IN_HBM,) * 3,
        [pltpu.VMEM((2,) + shape.shape, F32), pltpu.VMEM(dq.shape, F32), pltpu.SemaphoreType.DMA((3, tp_count))], 4,
        back, dq, dq_there,
    )
    return grad_query, key_gradient, value_gradient


def solution(mesh):
    return jax.shard_map(
        shards,
        mesh=mesh,
        in_specs=(P("ctx", "tp"), P(AXES, None), P(AXES, None), P("ctx", "tp")),
        out_specs=(P("ctx", "tp"), P(AXES, None), P(AXES, None)),
        check_vma=False,
    )
```
